128 devices in a mesh: section: 8 (over x_lo, y), tensor: 16 (over z, x_hi, core).
Axes of the slice: x: 4 (x_hi: 2, x_lo: 2; x = x_hi * 2 + x_lo), y: 4, z: 4, core: 2. Of those that a mesh axis runs over, the one named last changes fastest.
Arguments:
- hidden: bfloat16 [512, 4096], P('section', 'tensor'), may hold values from -24 to 24
- weight: bfloat16 [131072, 4096], P(('section', 'tensor')), may hold values from -1 to 1
- targets: int32 [512], replicated, may hold values from 0 to 131071
- loss_grad: float32 [512], replicated, may hold values from 4 to 16
Outputs:
- token_loss: float32 [512], replicated
- grad_hidden: bfloat16 [512, 4096], P('section', 'tensor')
- grad_weight: bfloat16 [131072, 4096], P(('section', 'tensor'))
The draws below stay inside these ranges and needn't reach their ends.
All inputs are finite; a program needn't handle non-finite values.
Results may differ from the reference program's by a relative error of at most 0.0047.
Values may be sent and summed in bfloat16 or wider, within the bound.
A program may use at most 64 MiB of HBM per device.

```python
import math
import jax
import jax.numpy as jnp

D = 4096
TOKENS = 512
VOCAB = 131072


def weight_rows(key, scale_low):
    noise_key = jax.random.fold_in(key, 11)
    scale_key = jax.random.fold_in(key, 12)
    normal_noise = jax.random.normal(noise_key, (VOCAB, D), jnp.float32)
    values_base = normal_noise
    row_scale = jnp.exp(jax.random.uniform(scale_key, (VOCAB,), jnp.float32, math.log(scale_low), 1e-09))
    rising = (0.75 + 0.5 * jnp.arange(VOCAB, dtype=jnp.float32) / VOCAB) * row_scale
    return jnp.clip(values_base * (rising * 3.0 / math.sqrt(D))[:, None], -1.0, 1.0)


def draw_weight(key, part):
    table = weight_rows(key, 1.0)
    return table.astype(jnp.bfloat16)


def draw_hidden(key, part):
    key = jax.random.fold_in(key, 3)
    values_base = jax.random.normal(jax.random.fold_in(key, 4), (TOKENS, D), jnp.float32)
    return jnp.clip(values_base, -24.0, 24.0).astype(jnp.bfloat16)


def place_ends(values, key, least, high):
    longest = values.shape.index(max(values.shape))
    spots = []
    for shift in (0, 1):
        where = [jax.random.randint(jax.random.fold_in(key, axis), (), 0, length) for axis, length in enumerate(values.shape)]
        where[longest] = (where[longest] + shift) % values.shape[longest]
        spots.append(tuple(where))
    return values.at[spots[0]].set(least).at[spots[1]].set(high)


def setup_inputs(seed: int = 0) -> dict:
    seeds = jax.random.split(jax.random.key(seed), 5)
    hidden = draw_hidden(jax.random.fold_in(seeds[4], 71), 0)
    weight = draw_weight(jax.random.fold_in(seeds[4], 71), 0)
    targets = place_ends(jax.random.randint(seeds[2], (TOKENS,), 0, VOCAB), jax.random.fold_in(seeds[2], 1), 0, VOCAB - 1).astype(jnp.int32)
    loss_grad = jnp.clip(jax.random.uniform(seeds[3], (TOKENS,), jnp.float32, 4.0, 16.0), 4.0, 16.0)
    return {"hidden": hidden, "weight": weight, "targets": targets, "loss_grad": loss_grad}


def reference(hidden, weight, targets, loss_grad):
    logits = jnp.dot(hidden, weight.T, preferred_element_type=jnp.float32)
    row_max = jnp.max(logits, axis=1)
    shifted = jnp.exp(logits - row_max[:, None])
    row_total = jnp.sum(shifted, axis=1)
    columns = jnp.arange(VOCAB, dtype=jnp.int32)
    target_mask = columns[None, :] == targets.astype(jnp.int32)[:, None]
    picked = jnp.sum(jnp.where(target_mask, logits, jnp.float32(0.0)), axis=1)
    token_loss = row_max + jnp.log(row_total) - picked
    grad_logits = (loss_grad[:, None] * (shifted / row_total[:, None] - target_mask.astype(jnp.float32))).astype(jnp.bfloat16)
    grad_weight = jnp.dot(grad_logits.T, hidden, preferred_element_type=jnp.float32).astype(jnp.bfloat16)
    grad_hidden = jnp.dot(grad_logits, weight, preferred_element_type=jnp.float32).astype(jnp.bfloat16)
    return (token_loss, grad_hidden, grad_weight)
```

```python
import jax
import jax.numpy as jnp
from jax import lax
from jax.experimental import pallas as pl
from jax.experimental.pallas import tpu as pltpu
from jax.sharding import PartitionSpec as P

MESH = pl.DeviceIdType.MESH
F32, BF16 = jnp.float32, jnp.bfloat16

ORDERS = ((0, 1, 2), (1, 2, 0), (2, 0, 1))
ROWS = ((0, 48), (48, 48), (96, 32))


def place():
    s, t = lax.axis_index("section"), lax.axis_index("tensor")
    return ((t // 2) % 2) * 2 + s // 4, s % 4, t // 4, t % 2


def device(x, y, z, c):
    return ((x % 2) * 4 + y, z * 4 + (x // 2) * 2 + c)


def region(at, rows=None):
    x, y, z = at
    whole = slice(None)
    ix = (
        whole if x is None else x % 2,
        whole if y is None else y,
        whole if z is None else z,
        whole if x is None else x // 2,
    )
    return ix if rows is None else ix + (pl.ds(rows[0], rows[1]),)


def moved(at, axis, delta):
    at = list(at)
    at[axis] = (at[axis] + delta) % 4
    return tuple(at)


def combine(parts):
    top = jnp.max(parts[:, 0], axis=0)
    total = jnp.sum(parts[:, 1] * jnp.exp(parts[:, 0] - top[None]), axis=0)
    return top, total, jnp.sum(parts[:, 2], axis=0)


def flat(rows):
    return jnp.concatenate([rows[i : i + 1] for i in range(4)], axis=1)


def kernel(
    hid_ref, w_hbm, tgt_ref, lg_ref,
    loss_ref, gh_ref, gw_ref,
    w, g, lt, glt, gl, own, give, take, r,
    rx1, ry1, rz1, rx2, ry2, rz2, r3a, r3b, r3c,
    st_core, st_plane, st_axis,
    w_sem, ag_s, ag_r, rel_s, rel_r, core_s, core_r, rs_s, rs_r,
    sc_s, sc_r, sp_s, sp_r, sa_s, sa_r,
):
    x, y, z, c = place()
    me = (x, y, z)
    vocab, depth = w.shape
    tokens = lt.shape[1]
    partner = device(x, y, z, 1 - c)

    load_w = pltpu.make_async_copy(w_hbm, w, w_sem)
    load_w.start()

    own_g = (c,) + region(me)
    g[own_g + (pl.ds(0, 64),)] = hid_ref[:, 0:128]
    g[own_g + (pl.ds(64, 64),)] = hid_ref[:, 128:256]

    barrier = pltpu.get_barrier_semaphore()
    peers = [partner]
    for dx in range(4):
        for dy in range(4):
            if dx or dy:
                peers.append(device((x + dx) % 4, (y + dy) % 4, z, c))
    for dz in range(1, 4):
        peers.append(device(x, y, (z + dz) % 4, c))
    for peer in peers:
        pl.semaphore_signal(barrier, inc=1, device_id=peer, device_id_type=MESH)
    pl.semaphore_wait(barrier, len(peers))

    sends = {}
    relays = []

    def send(k, p, d):
        axis = ORDERS[k][p]
        at = tuple(None if a in ORDERS[k][:p] else me[a] for a in range(3))
        ref = g.at[(c,) + region(at, ROWS[k])]
        i = (k * 3 + p) * 3 + d - 1
        cp = pltpu.make_async_remote_copy(
            ref, ref, ag_s.at[i], ag_r.at[i],
            device_id=device(*moved(me, axis, d), c), device_id_type=MESH,
        )
        cp.start()
        sends[k, p, d] = cp

    def relay(k, d):
        axis = ORDERS[k][2]
        at = tuple((me[a] - d) % 4 if a == axis else None for a in range(3))
        ref = g.at[(c,) + region(at, ROWS[k])]
        i = k * 4 + d
        cp = pltpu.make_async_remote_copy(
            ref, ref, rel_s.at[i], rel_r.at[i], device_id=partner, device_id_type=MESH
        )
        cp.start()
        relays.append(cp)

    for k in range(3):
        for d in (1, 3, 2):
            send(k, 0, d)
    for p in (1, 2):
        for k in range(3):
            for d in (1, 3, 2):
                sends[k, p - 1, d].wait_recv()
            for d in (1, 3, 2):
                send(k, p, d)
    for k in range(3):
        relay(k, 0)
    for d in (1, 3, 2):
        for k in range(3):
            sends[k, 2, d].wait_recv()
            relay(k, d)
    for cp in relays:
        cp.wait_recv()
    load_w.wait()

    def features(q):
        zz, xx = q // 2, q % 2
        parts = [
            g[cc, :, :, zz, xx, pl.ds(64 * h, 64), :].reshape(tokens, 128)
            for cc in range(2)
            for h in range(2)
        ]
        return jnp.concatenate(parts, axis=1)

    def columns(q, width=512):
        return pl.ds(pl.multiple_of(q * width, width), width)

    lt[...] = jnp.zeros_like(lt)

    def logit_step(q, _):
        rhs = features(q)
        for i in range(4):
            rows = pl.ds(i * (vocab // 4), vocab // 4)
            lt[rows, :] += lax.dot_general(
                w[rows, columns(q)], rhs, (((1,), (1,)), ((), ())),
                preferred_element_type=F32,
            )
        return 0

    lax.fori_loop(0, 8, logit_step, 0)

    s_idx, t_idx = lax.axis_index("section"), lax.axis_index("tensor")
    local = tgt_ref[...] - (s_idx * 16 + t_idx) * vocab
    chunk = 64
    n_chunks = vocab // chunk

    def hit(i):
        ids = lax.broadcasted_iota(jnp.int32, (chunk, tokens), 0) + i * chunk
        return ids == local

    def max_step(i, top):
        return jnp.maximum(top, lt[pl.ds(pl.multiple_of(i * chunk, chunk), chunk), :])

    top = lax.fori_loop(1, n_chunks, max_step, lt[pl.ds(0, chunk), :])
    top = jnp.max(top, axis=0, keepdims=True)

    def exp_step(i, carry):
        total, picked = carry
        rows = pl.ds(pl.multiple_of(i * chunk, chunk), chunk)
        value = lt[rows, :]
        e = jnp.exp(value - top)
        lt[rows, :] = e
        picked = picked + jnp.sum(jnp.where(hit(i), value, 0.0), axis=0, keepdims=True)
        return total + jnp.sum(e, axis=0, keepdims=True), picked

    zero = jnp.zeros((1, tokens), F32)
    total, picked = lax.fori_loop(0, n_chunks, exp_step, (zero, zero))

    for j, v in enumerate((top, total, picked)):
        for i in range(4):
            st_core[0, j, i : i + 1, :] = v[:, 128 * i : 128 * (i + 1)]
    core_copy = pltpu.make_async_remote_copy(
        st_core.at[0], st_core.at[1], sc_s, sc_r, device_id=partner, device_id_type=MESH
    )
    core_copy.start()
    core_copy.wait_recv()
    for j, v in enumerate(combine(st_core[...])):
        st_plane[0, j] = v
    plane_copies = []
    for dx in range(4):
        for dy in range(4):
            i = dx * 4 + dy
            if i:
                cp = pltpu.make_async_remote_copy(
                    st_plane.at[0], st_plane.at[i], sp_s.at[i], sp_r.at[i],
                    device_id=device((x + dx) % 4, (y + dy) % 4, z, c),
                    device_id_type=MESH,
                )
                cp.start()
                plane_copies.append(cp)
    for cp in plane_copies:
        cp.wait_recv()
    for j, v in enumerate(combine(st_plane[...])):
        st_axis[0, j] = v
    axis_copies = []
    for d in (1, 3, 2):
        cp = pltpu.make_async_remote_copy(
            st_axis.at[0], st_axis.at[d], sa_s.at[d], sa_r.at[d],
            device_id=device(x, y, (z + d) % 4, c), device_id_type=MESH,
        )
        cp.start()
        axis_copies.append(cp)
    for cp in axis_copies:
        cp.wait_recv()
    m_all, s_all, p_all = combine(st_axis[...])
    loss_ref[...] = m_all + jnp.log(s_all) - p_all
    lg = lg_ref[...]
    scale = lg * jnp.exp(top - flat(m_all)) / flat(s_all)

    def grad_step(i, _):
        rows = pl.ds(pl.multiple_of(i * chunk, chunk), chunk)
        value = lt[rows, :] * scale - jnp.where(hit(i), lg, 0.0)
        glt[rows, :] = value.astype(BF16)
        return 0

    lax.fori_loop(0, n_chunks, grad_step, 0)
    for i in range(8):
        gl[:, 128 * i : 128 * (i + 1)] = glt[128 * i : 128 * (i + 1), :].T

    def term(t):
        return jnp.dot(gl[...], w[:, columns(t, 256)], preferred_element_type=F32)

    def core_send(q):
        zz, xx = q // 2, q % 2
        return pltpu.make_async_remote_copy(
            give.at[q], take.at[q], core_s.at[q], core_r.at[q],
            device_id=partner, device_id_type=MESH,
        )

    def join(q):
        zz, xx = q // 2, q % 2
        core_send(q).wait_recv()
        r[:, :, zz, xx] = (own[q].astype(F32) + take[q].astype(F32)).astype(BF16)

    def term_step(q, _):
        value = term(q * 2 + 1 - c).astype(BF16)
        give[q, :, :, 0:64] = value[:, 0:128].reshape(2, 4, 64, 128)
        give[q, :, :, 64:128] = value[:, 128:256].reshape(2, 4, 64, 128)
        core_send(q).start()
        value = term(q * 2 + c)
        own[q, :, :, 0:64] = value[:, 0:128].reshape(2, 4, 64, 128)
        own[q, :, :, 64:128] = value[:, 128:256].reshape(2, 4, 64, 128)
        pl.when(q > 0)(lambda: join(q - 1))
        return 0

    lax.fori_loop(0, 8, term_step, 0)
    join(7)

    slots = ((rz1, ry2, r3a), (rx1, rz2, r3b), (ry1, rx2, r3c))
    rs = {}

    def rs_send(k, p):
        axis = ORDERS[k][2 - p]
        for d in (1, 3, 2):
            at = tuple(
                (me[a] + d) % 4 if a == axis else None if a in ORDERS[k][: 2 - p] else me[a]
                for a in range(3)
            )
            i = (k * 3 + p) * 3 + d - 1
            cp = pltpu.make_async_remote_copy(
                r.at[region(at, ROWS[k])], slots[k][p].at[d - 1], rs_s.at[i], rs_r.at[i],
                device_id=device(*moved(me, axis, d), c), device_id_type=MESH,
            )
            cp.start()
            rs[k, p, d] = cp

    def rs_sum(k, p):
        axis = ORDERS[k][2 - p]
        at = tuple(None if a in ORDERS[k][: 2 - p] else me[a] for a in range(3))
        ix = region(at, ROWS[k])
        value = r[ix].astype(F32)
        for d in (1, 3, 2):
            rs[k, p, d].wait_recv()
            value = value + slots[k][p][d - 1].astype(F32)
        r[ix] = value.astype(BF16)

    def weight_step(q, _):
        gw_ref[:, columns(q)] = jnp.dot(
            glt[...], features(q), preferred_element_type=F32
        ).astype(BF16)
        return 0

    for k in range(3):
        rs_send(k, 0)
    lax.fori_loop(0, 4, weight_step, 0)
    for k in range(3):
        rs_sum(k, 0)
        rs_send(k, 1)
    lax.fori_loop(4, 6, weight_step, 0)
    for k in range(3):
        rs_sum(k, 1)
        rs_send(k, 2)
    lax.fori_loop(6, 8, weight_step, 0)
    for k in range(3):
        rs_sum(k, 2)
    mine = region(me)
    gh_ref[:, 0:128] = r[mine + (pl.ds(0, 64),)]
    gh_ref[:, 128:256] = r[mine + (pl.ds(64, 64),)]

    for cp in (
        list(sends.values()) + relays + [core_copy] + plane_copies + axis_copies + list(rs.values())
    ):
        cp.wait_send()

    def drain(q, _):
        core_send(q).wait_send()
        return 0

    lax.fori_loop(0, 8, drain, 0)


def write_kernel(src, dst, sem):
    cp = pltpu.make_async_copy(src, dst, sem)
    cp.start()
    cp.wait()


def shards(hidden, weight, targets, loss_grad):
    vocab, depth = weight.shape
    tokens = targets.shape[0]
    dma = pltpu.SemaphoreType.DMA
    vmem = pl.BlockSpec(memory_space=pltpu.VMEM)
    slot = lambda *s: pltpu.VMEM((3,) + s + (128,), BF16)
    loss, grad_hidden, grad_weight = pl.pallas_call(
        kernel,
        out_shape=(
            jax.ShapeDtypeStruct((4, 128), F32),
            jax.ShapeDtypeStruct(hidden.shape, BF16),
            pltpu.VMEM((vocab, depth), BF16),
        ),
        in_specs=[vmem, pl.BlockSpec(memory_space=pl.ANY), vmem, vmem],
        out_specs=(vmem, vmem, vmem),
        scratch_shapes=[
            pltpu.VMEM((vocab, depth), BF16),
            pltpu.VMEM((2, 2, 4, 4, 2, 128, 128), BF16),
            pltpu.VMEM((vocab, tokens), F32),
            pltpu.VMEM((vocab, tokens), BF16),
            pltpu.VMEM((tokens, vocab), BF16),
            pltpu.VMEM((8, 2, 4, 128, 128), F32),
            pltpu.VMEM((8, 2, 4, 128, 128), BF16),
            pltpu.VMEM((8, 2, 4, 128, 128), BF16),
            pltpu.VMEM((2, 4, 4, 2, 128, 128), BF16),
            slot(4, 4, 48), slot(2, 4, 2, 32), slot(2, 4, 2, 48),
            slot(4, 32), slot(2, 2, 48), slot(4, 48),
            slot(48), slot(48), slot(32),
            pltpu.VMEM((2, 3, 4, 128), F32),
            pltpu.VMEM((16, 3, 4, 128), F32),
            pltpu.VMEM((4, 3, 4, 128), F32),
            dma,
            dma((27,)), dma((27,)), dma((12,)), dma((12,)),
            dma((8,)), dma((8,)), dma((27,)), dma((27,)),
            dma, dma, dma((16,)), dma((16,)), dma((4,)), dma((4,)),
        ],
        compiler_params=pltpu.CompilerParams(
            collective_id=0, has_side_effects=True, vmem_limit_bytes=50 * 2**20
        ),
    )(hidden, weight, targets.reshape(1, tokens), loss_grad.reshape(1, tokens))
    grad_weight = pl.pallas_call(
        write_kernel,
        out_shape=jax.ShapeDtypeStruct((vocab, depth), BF16),
        in_specs=[vmem],
        out_specs=pl.BlockSpec(memory_space=pl.ANY),
        scratch_shapes=[dma],
        compiler_params=pltpu.CompilerParams(vmem_limit_bytes=16 * 2**20),
    )(grad_weight)
    return loss.reshape(tokens), grad_hidden, grad_weight


def solution(mesh):
    return jax.shard_map(
        shards,
        mesh=mesh,
        in_specs=(P("section", "tensor"), P(("section", "tensor"), None), P(), P()),
        out_specs=(P(), P("section", "tensor"), P(("section", "tensor"), None)),
        check_vma=False,
    )
```

```python
import jax
import jax.numpy as jnp
from jax import lax
from jax.experimental import pallas as pl
from jax.experimental.pallas import tpu as pltpu
from jax.sharding import PartitionSpec as P

MESH = pl.DeviceIdType.MESH
F32, BF16 = jnp.float32, jnp.bfloat16
X, Y, Z = 0, 1, 2

ORDERS = ((X, Y, Z), (Y, Z, X), (X, Z, Y))
ROWS = ((0, 32), (32, 48), (80, 48))
NEAR = (1, 3, 2)
COPIES = 134


def place():
    s, t = lax.axis_index("section"), lax.axis_index("tensor")
    return ((t // 2) % 2) * 2 + s // 4, s % 4, t // 4, t % 2


def device(x, y, z, c):
    return ((x % 2) * 4 + y, z * 4 + (x // 2) * 2 + c)


def region(at, rows=None):
    x, y, z = at
    whole = slice(None)
    ix = (
        whole if x is None else x % 2,
        whole if y is None else y,
        whole if z is None else z,
        whole if x is None else x // 2,
    )
    return ix if rows is None else ix + (pl.ds(rows[0], rows[1]),)


def combine(parts):
    top = jnp.max(parts[:, 0], axis=0)
    total = jnp.sum(parts[:, 1] * jnp.exp(parts[:, 0] - top[None]), axis=0)
    return top, total, jnp.sum(parts[:, 2], axis=0)


def flat(rows):
    return jnp.concatenate([rows[i : i + 1] for i in range(4)], axis=1)


def kernel(
    hid_ref, w_hbm, tgt_ref, lg_ref,
    loss_ref, gh_ref, gw_ref,
    w, g, lt, glt, gl, own, give, take, r,
    a0, b0, c0, a1, b1, c1, a2, b2, c2, fa, fb, fc,
    st_core, st_plane, st_axis,
    w_sem, send_sem, recv_sem,
):
    x, y, z, c = place()
    me = (x, y, z)
    vocab, depth = w.shape
    tokens = lt.shape[1]
    partner = device(x, y, z, 1 - c)

    load_w = pltpu.make_async_copy(w_hbm, w, w_sem)
    load_w.start()

    own_g = (c,) + region(me)
    g[own_g + (pl.ds(0, 64),)] = hid_ref[:, 0:128]
    g[own_g + (pl.ds(64, 64),)] = hid_ref[:, 128:256]

    barrier = pltpu.get_barrier_semaphore()
    peers = [partner]
    for dx in range(4):
        for dy in range(4):
            if dx or dy:
                peers.append(device((x + dx) % 4, (y + dy) % 4, z, c))
    for dz in range(1, 4):
        peers.append(device(x, y, (z + dz) % 4, c))
    for peer in peers:
        pl.semaphore_signal(barrier, inc=1, device_id=peer, device_id_type=MESH)
    lt[...] = jnp.zeros_like(lt)
    pl.semaphore_wait(barrier, len(peers))

    copies = []

    def send(src, dst, to):
        i = len(copies)
        cp = pltpu.make_async_remote_copy(
            src, dst, send_sem.at[i], recv_sem.at[i], device_id=to, device_id_type=MESH
        )
        cp.start()
        copies.append(cp)
        return cp

    def peer(axis, d):
        return device(*[(me[a] + d) % 4 if a == axis else me[a] for a in range(3)], c)

    def spot(k, **at):
        out = [None, None, None]
        for name, axis in zip(("first", "second", "last"), ORDERS[k]):
            d = at.get(name, 0)
            out[axis] = None if d == "all" else (me[axis] + d) % 4
        return tuple(out)

    def spread(k, role, d, **at):
        ref = g.at[(c,) + region(spot(k, **at), ROWS[k])]
        return send(ref, ref, peer(ORDERS[k][role], d))

    got0, got1, got2 = {}, {}, {}
    for k in range(3):
        for d in NEAR:
            got0[k, d] = spread(k, 0, d)
    for k in range(3):
        for d in NEAR:
            got0[k, d].wait_recv()
        for d in NEAR:
            got1[k, d] = spread(k, 1, d, first="all")
    for k in range(3):
        for d in NEAR:
            got2[k, 0, d] = spread(k, 2, d, first="all")
    for s in NEAR:
        for k in range(3):
            got1[k, s].wait_recv()
            for d in NEAR:
                got2[k, s, d] = spread(k, 2, d, first="all", second=-s)

    def relay(s):
        done = []
        for k in range(3):
            if k == 0:
                if s:
                    for i in (0,) + NEAR:
                        got2[0, i, s].wait_recv()
            else:
                for d in NEAR:
                    got2[k, s, d].wait_recv()
            ref = g.at[(c,) + region((None, None, (z - s) % 4), ROWS[k])]
            done.append(send(ref, ref, partner))
        return done

    def features(zz):
        parts = [
            g[cc, :, :, zz, xx, pl.ds(64 * h, 64), :].reshape(tokens, 128)
            for xx in range(2)
            for cc in range(2)
            for h in range(2)
        ]
        return jnp.concatenate(parts, axis=1)

    def columns(i, width):
        return pl.ds(pl.multiple_of(i * width, width), width)

    def logits(s):
        zz = (z - s) % 4

        def step(i, _):
            rows = columns(i, 256)
            lt[rows, :] += lax.dot_general(
                w[rows, columns(zz, 1024)], features(zz), (((1,), (1,)), ((), ())),
                preferred_element_type=F32,
            )
            return 0

        lax.fori_loop(0, vocab // 256, step, 0)

    relayed = relay(0)
    load_w.wait()
    before = 0
    for s in NEAR:
        upcoming = relay(s)
        for cp in relayed:
            cp.wait_recv()
        logits(before)
        relayed, before = upcoming, s
    for cp in relayed:
        cp.wait_recv()
    logits(before)

    s_idx, t_idx = lax.axis_index("section"), lax.axis_index("tensor")
    local = tgt_ref[...] - (s_idx * 16 + t_idx) * vocab
    chunk = 64
    n_chunks = vocab // chunk

    def hit(i):
        ids = lax.broadcasted_iota(jnp.int32, (chunk, tokens), 0) + i * chunk
        return ids == local

    def max_step(i, top):
        return jnp.maximum(top, lt[pl.ds(pl.multiple_of(i * chunk, chunk), chunk), :])

    top = lax.fori_loop(1, n_chunks, max_step, lt[pl.ds(0, chunk), :])
    top = jnp.max(top, axis=0, keepdims=True)

    def exp_step(i, carry):
        total, picked = carry
        rows = pl.ds(pl.multiple_of(i * chunk, chunk), chunk)
        value = lt[rows, :]
        e = jnp.exp(value - top)
        lt[rows, :] = e
        picked = picked + jnp.sum(jnp.where(hit(i), value, 0.0), axis=0, keepdims=True)
        return total + jnp.sum(e, axis=0, keepdims=True), picked

    zero = jnp.zeros((1, tokens), F32)
    total, picked = lax.fori_loop(0, n_chunks, exp_step, (zero, zero))

    for j, v in enumerate((top, total, picked)):
        for i in range(4):
            st_core[0, j, i : i + 1, :] = v[:, 128 * i : 128 * (i + 1)]
    send(st_core.at[0], st_core.at[1], partner).wait_recv()
    for j, v in enumerate(combine(st_core[...])):
        st_plane[0, j] = v
    joined = []
    for dx in range(4):
        for dy in range(4):
            i = dx * 4 + dy
            if i:
                to = device((x + dx) % 4, (y + dy) % 4, z, c)
                joined.append(send(st_plane.at[0], st_plane.at[i], to))
    for cp in joined:
        cp.wait_recv()
    for j, v in enumerate(combine(st_plane[...])):
        st_axis[0, j] = v
    joined = [send(st_axis.at[0], st_axis.at[d], peer(Z, d)) for d in NEAR]
    for cp in joined:
        cp.wait_recv()
    m_all, s_all, p_all = combine(st_axis[...])
    loss_ref[...] = m_all + jnp.log(s_all) - p_all
    lg = lg_ref[...]
    scale = lg * jnp.exp(top - flat(m_all)) / flat(s_all)

    def grad_step(i, _):
        rows = pl.ds(pl.multiple_of(i * chunk, chunk), chunk)
        value = lt[rows, :] * scale - jnp.where(hit(i), lg, 0.0)
        glt[rows, :] = value.astype(BF16)
        return 0

    lax.fori_loop(0, n_chunks, grad_step, 0)
    for i in range(8):
        gl[:, 128 * i : 128 * (i + 1)] = glt[128 * i : 128 * (i + 1), :].T

    def term(zz, xx, cc, out):
        t = (zz * 2 + xx) * 2 + cc
        value = jnp.dot(gl[...], w[:, columns(t, 256)], preferred_element_type=F32)
        value = value.astype(out.dtype)
        out[xx, :, :, 0:64] = value[:, 0:128].reshape(2, 4, 64, 128)
        out[xx, :, :, 64:128] = value[:, 128:256].reshape(2, 4, 64, 128)

    def both(zz, cc, out):
        def step(xx, _):
            term(zz, xx, cc, out)
            return 0

        lax.fori_loop(0, 2, step, 0)

    def swap(i, s):
        both((z + s) % 4, 1 - c, give.at[i])
        return send(give.at[i], take.at[i], partner)

    slots0, slots1, slots2 = (a0, b0, c0), (a1, b1, c1), (a2, b2, c2)
    finals = (fa, fb, fc)
    red0, red1, red2 = {}, {}, {}

    def reduce_z(s):
        if s:
            ref = r.at[region(spot(0, first="all", second="all", last=s), ROWS[0])]
            red0[0, s] = send(ref, a0.at[s - 1], peer(Z, s))
        for k in (1, 2):
            for d in NEAR:
                ref = r.at[region(spot(k, first="all", second=s, last=d), ROWS[k])]
                red0[k, s, d] = send(ref, slots0[k].at[s, d - 1], peer(ORDERS[k][2], d))

    def line(k, s):
        ix = region(spot(k, first="all", second=s), ROWS[k])
        value = r[ix].astype(F32)
        for d in NEAR:
            if k == 0:
                value = value + a0[d - 1, :, (y + s) % 4].astype(F32)
            else:
                red0[k, s, d].wait_recv()
                value = value + slots0[k][s, d - 1].astype(F32)
        return ix, value

    def pass_line(k, s):
        ix, value = line(k, s)
        r[ix] = value.astype(BF16)
        red1[k, s] = send(r.at[ix], slots1[k].at[s - 1], peer(ORDERS[k][1], s))

    def own_line(k):
        value = line(k, 0)[1]
        for d in NEAR:
            red1[k, d].wait_recv()
            value = value + slots1[k][d - 1].astype(F32)
        finals[k][...] = value
        axis = ORDERS[k][0]
        for d in NEAR:
            n = (me[axis] + d) % 4
            ref = finals[k].at[(n % 2, n // 2) if axis == X else (n,)]
            red2[k, d] = send(ref, slots2[k].at[d - 1], peer(axis, d))

    def weight_grad(start, stop):
        def step(i, _):
            for h in range(2):
                rows = slice(512 * h, 512 * (h + 1))
                gw_ref[rows, columns(i, 1024)] = jnp.dot(
                    glt[rows, :], features(i), preferred_element_type=F32
                ).astype(BF16)
            return 0

        lax.fori_loop(start, stop, step, 0)

    turns = NEAR + (0,)
    swaps = [swap(0, turns[0])]
    for i, s in enumerate(turns):
        if i < 3:
            swaps.append(swap(i + 1, turns[i + 1]))
        both((z + s) % 4, c, own)
        swaps[i].wait_recv()
        for xx in range(2):
            r[:, :, (z + s) % 4, xx] = (own[xx] + take[i, xx].astype(F32)).astype(BF16)
        reduce_z(s)
    weight_grad(0, 1)
    for k in (1, 2):
        pass_line(k, 1)
    weight_grad(1, 2)
    for k in (1, 2):
        pass_line(k, 3)
    weight_grad(2, 3)
    for d in NEAR:
        red0[0, d].wait_recv()
    for s in NEAR:
        pass_line(0, s)
    for k in (1, 2):
        pass_line(k, 2)
    weight_grad(3, 4)
    for k in range(3):
        own_line(k)
    mine = region(me)
    for k in range(3):
        axis = ORDERS[k][0]
        n = me[axis]
        value = finals[k][(n % 2, n // 2) if axis == X else (n,)]
        for d in NEAR:
            red2[k, d].wait_recv()
            value = value + slots2[k][d - 1]
        r[region(me, ROWS[k])] = value.astype(BF16)
    gh_ref[:, 0:128] = r[mine + (pl.ds(0, 64),)]
    gh_ref[:, 128:256] = r[mine + (pl.ds(64, 64),)]

    assert len(copies) == COPIES, len(copies)
    for cp in copies:
        cp.wait_send()


def write_kernel(gw, loss, gh, gw_out, loss_out, gh_out, sem):
    pairs = ((gw, gw_out), (loss, loss_out), (gh, gh_out))
    copies = [pltpu.make_async_copy(a, b, sem.at[i]) for i, (a, b) in enumerate(pairs)]
    for cp in copies:
        cp.start()
    for cp in copies:
        cp.wait()


def shards(hidden, weight, targets, loss_grad):
    vocab, depth = weight.shape
    tokens = targets.shape[0]
    dma = pltpu.SemaphoreType.DMA
    vmem = pl.BlockSpec(memory_space=pltpu.VMEM)
    anywhere = pl.BlockSpec(memory_space=pl.ANY)
    slot = lambda *s, t=BF16: pltpu.VMEM(s + (128,), t)
    loss, grad_hidden, grad_weight = pl.pallas_call(
        kernel,
        out_shape=(
            pltpu.VMEM((4, 128), F32),
            pltpu.VMEM(hidden.shape, BF16),
            pltpu.VMEM((vocab, depth), BF16),
        ),
        in_specs=[vmem, anywhere, vmem, vmem],
        out_specs=(vmem, vmem, vmem),
        scratch_shapes=[
            pltpu.VMEM((vocab, depth), BF16),
            pltpu.VMEM((2, 2, 4, 4, 2, 128, 128), BF16),
            pltpu.VMEM((vocab, tokens), F32),
            pltpu.VMEM((vocab, tokens), BF16),
            pltpu.VMEM((tokens, vocab), BF16),
            pltpu.VMEM((2, 2, 4, 128, 128), F32),
            pltpu.VMEM((4, 2, 2, 4, 128, 128), BF16),
            pltpu.VMEM((4, 2, 2, 4, 128, 128), BF16),
            pltpu.VMEM((2, 4, 4, 2, 128, 128), BF16),
            slot(3, 2, 4, 2, 32), slot(4, 3, 4, 48), slot(4, 3, 2, 2, 48),
            slot(3, 2, 2, 32), slot(3, 4, 48), slot(3, 2, 2, 48),
            slot(3, 32, t=F32), slot(3, 48, t=F32), slot(3, 48, t=F32),
            slot(2, 2, 32, t=F32), slot(4, 48, t=F32), slot(2, 2, 48, t=F32),
            pltpu.VMEM((2, 3, 4, 128), F32),
            pltpu.VMEM((16, 3, 4, 128), F32),
            pltpu.VMEM((4, 3, 4, 128), F32),
            dma, dma((COPIES,)), dma((COPIES,)),
        ],
        compiler_params=pltpu.CompilerParams(
            collective_id=0, has_side_effects=True, vmem_limit_bytes=48 * 2**20
        ),
    )(hidden, weight, targets.reshape(1, tokens), loss_grad.reshape(1, tokens))
    grad_weight, loss, grad_hidden = pl.pallas_call(
        write_kernel,
        out_shape=(
            jax.ShapeDtypeStruct((vocab, depth), BF16),
            jax.ShapeDtypeStruct((4, 128), F32),
            jax.ShapeDtypeStruct(hidden.shape, BF16),
        ),
        in_specs=[vmem] * 3,
        out_specs=(anywhere,) * 3,
        scratch_shapes=[dma((3,))],
        compiler_params=pltpu.CompilerParams(vmem_limit_bytes=16 * 2**20),
    )(grad_weight, loss, grad_hidden)
    return loss.reshape(tokens), grad_hidden, grad_weight


def solution(mesh):
    return jax.shard_map(
        shards,
        mesh=mesh,
        in_specs=(P("section", "tensor"), P(("section", "tensor"), None), P(), P()),
        out_specs=(P(), P("section", "tensor"), P(("section", "tensor"), None)),
        check_vma=False,
    )
```

```python
import jax
import jax.numpy as jnp
from jax import lax
from jax.experimental import pallas as pl
from jax.experimental.pallas import tpu as pltpu
from jax.sharding import PartitionSpec as P

MESH = pl.DeviceIdType.MESH
F32, BF16 = jnp.float32, jnp.bfloat16
X, Y, Z = 0, 1, 2

ORDERS = ((X, Y, Z), (Y, Z, X), (X, Z, Y))
ROWS = ((0, 32), (32, 48), (80, 48))
NEAR = (1, 3, 2)
COPIES = 191
PIECES = 8


def place():
    s, t = lax.axis_index("section"), lax.axis_index("tensor")
    return ((t // 2) % 2) * 2 + s // 4, s % 4, t // 4, t % 2


def device(x, y, z, c):
    return ((x % 2) * 4 + y, z * 4 + (x // 2) * 2 + c)


def region(at, rows=None):
    x, y, z = at
    whole = slice(None)
    ix = (
        whole if x is None else x % 2,
        whole if y is None else y,
        whole if z is None else z,
        whole if x is None else x // 2,
    )
    return ix if rows is None else ix + (pl.ds(rows[0], rows[1]),)


def combine(parts):
    top = jnp.max(parts[:, 0], axis=0)
    total = jnp.sum(parts[:, 1] * jnp.exp(parts[:, 0] - top[None]), axis=0)
    return top, total, jnp.sum(parts[:, 2], axis=0)


def flat(rows):
    return jnp.concatenate([rows[i : i + 1] for i in range(4)], axis=1)


def kernel(
    hid_ref, w_hbm, tgt_ref, lg_ref,
    loss_ref, gh_ref, gw_ref,
    w, g, lt, glt, gl, own, give, take, r,
    a0, b0, c0, a1, b1, c1, fa, fb, fc,
    st_plane, st_axis,
    w_sem, send_sem, recv_sem,
):
    x, y, z, c = place()
    me = (x, y, z)
    vocab, depth = w.shape
    tokens = lt.shape[1]
    partner = device(x, y, z, 1 - c)

    def there(moves, cc=c):
        return device(*[(me[a] + moves.get(a, 0)) % 4 for a in range(3)], cc)

    load_w = pltpu.make_async_copy(w_hbm, w, w_sem)
    load_w.start()

    own_g = (c,) + region(me)
    g[own_g + (pl.ds(0, 64),)] = hid_ref[:, 0:128]
    g[own_g + (pl.ds(64, 64),)] = hid_ref[:, 128:256]

    barrier = pltpu.get_barrier_semaphore()
    peers = [partner]
    for d in NEAR:
        peers += [there({axis: d}) for axis in (X, Y, Z)] + [there({Z: d}, 1 - c)]
        peers += [there({p: d, q: e}) for p, q in ((X, Y), (Y, Z), (X, Z)) for e in NEAR]
    for to in peers:
        pl.semaphore_signal(barrier, inc=1, device_id=to, device_id_type=MESH)
    lt[...] = jnp.zeros_like(lt)
    pl.semaphore_wait(barrier, len(peers))

    copies = []

    def send(src, dst, to):
        i = len(copies)
        cp = pltpu.make_async_remote_copy(
            src, dst, send_sem.at[i], recv_sem.at[i], device_id=to, device_id_type=MESH
        )
        cp.start()
        copies.append(cp)
        return cp

    def spot(k, **at):
        out = [None, None, None]
        for name, axis in zip(("first", "second", "last"), ORDERS[k]):
            d = at.get(name, 0)
            out[axis] = None if d == "all" else (me[axis] + d) % 4
        return tuple(out)

    def spread(k, to, **at):
        ref = g.at[(c,) + region(spot(k, **at), ROWS[k])]
        return send(ref, ref, to)

    got1, got2 = {}, {}
    for s in (0,) + NEAR:
        for k in range(3):
            for d in (0,) + NEAR:
                if s or d:
                    got1[k, s, d] = spread(k, there({ORDERS[k][0]: d, ORDERS[k][1]: s}))
    for s in (0,) + NEAR:
        for k in range(3):
            for d in (0,) + NEAR:
                if s or d:
                    got1[k, s, d].wait_recv()
            for d in NEAR:
                got2[k, s, d] = spread(k, there({ORDERS[k][2]: d}), first="all", second=-s)

    def relay(s):
        done = []
        for k in range(3):
            if k == 0:
                if s:
                    for i in (0,) + NEAR:
                        got2[0, i, s].wait_recv()
            else:
                for d in NEAR:
                    got2[k, s, d].wait_recv()
            ref = g.at[(c,) + region((None, None, (z - s) % 4), ROWS[k])]
            done.append(send(ref, ref, partner))
        return done

    def features(zz, classes=(0, 1)):
        parts = [
            g[cc, :, :, zz, xx, pl.ds(64 * h, 64), :].reshape(tokens, 128)
            for xx in range(2)
            for cc in classes
            for h in range(2)
        ]
        return jnp.concatenate(parts, axis=1)

    def columns(i, width):
        return pl.ds(pl.multiple_of(i * width, width), width)

    def logits(s, cc=None):
        zz = (z - s) % 4
        if cc is None:
            part, rhs = w[:, columns(zz, 1024)], features(zz)
        else:
            part = jnp.concatenate([w[:, columns((zz * 2 + xx) * 2 + cc, 256)] for xx in range(2)], axis=1)
            rhs = features(zz, (cc,))
        lt[...] += lax.dot_general(
            part, rhs, (((1,), (1,)), ((), ())), preferred_element_type=F32
        )

    def arrived(relayed):
        for cp in relayed:
            cp.wait_recv()

    relayed = {0: relay(0)}
    load_w.wait()
    arrived(relayed[0])
    logits(0)
    for s in NEAR:
        relayed[s] = relay(s)
    logits(1, c)
    arrived(relayed[1])
    logits(1, 1 - c)
    arrived(relayed[3])
    logits(3)
    arrived(relayed[2])
    logits(2)

    s_idx, t_idx = lax.axis_index("section"), lax.axis_index("tensor")
    local = tgt_ref[...] - (s_idx * 16 + t_idx) * vocab
    chunk = 64
    n_chunks = vocab // chunk

    def hit(i):
        ids = lax.broadcasted_iota(jnp.int32, (chunk, tokens), 0) + i * chunk
        return ids == local

    def max_step(i, top):
        return jnp.maximum(top, lt[pl.ds(pl.multiple_of(i * chunk, chunk), chunk), :])

    top = lax.fori_loop(1, n_chunks, max_step, lt[pl.ds(0, chunk), :])
    top = jnp.max(top, axis=0, keepdims=True)

    def exp_step(i, carry):
        total, picked = carry
        rows = pl.ds(pl.multiple_of(i * chunk, chunk), chunk)
        value = lt[rows, :]
        e = jnp.exp(value - top)
        lt[rows, :] = e
        picked = picked + jnp.sum(jnp.where(hit(i), value, 0.0), axis=0, keepdims=True)
        return total + jnp.sum(e, axis=0, keepdims=True), picked

    zero = jnp.zeros((1, tokens), F32)
    total, picked = lax.fori_loop(0, n_chunks, exp_step, (zero, zero))

    for j, v in enumerate((top, total, picked)):
        for i in range(4):
            st_plane[0, j, i : i + 1, :] = v[:, 128 * i : 128 * (i + 1)]
    joined = []
    for dx in range(4):
        for dy in range(4):
            i = dx * 4 + dy
            if i:
                joined.append(send(st_plane.at[0], st_plane.at[i], there({X: dx, Y: dy})))
    for cp in joined:
        cp.wait_recv()
    for j, v in enumerate(combine(st_plane[...])):
        st_axis[0, j] = v
    joined = [
        send(st_axis.at[0], st_axis.at[d * 2 + i], there({Z: d}, cc))
        for i, cc in enumerate((c, 1 - c))
        for d in (0,) + NEAR
        if d or i
    ]
    for cp in joined:
        cp.wait_recv()
    m_all, s_all, p_all = combine(st_axis[...])
    loss_ref[...] = m_all + jnp.log(s_all) - p_all
    lg = lg_ref[...]
    scale = lg * jnp.exp(top - flat(m_all)) / flat(s_all)

    def grad_step(i, _):
        rows = pl.ds(pl.multiple_of(i * chunk, chunk), chunk)
        value = lt[rows, :] * scale - jnp.where(hit(i), lg, 0.0)
        glt[rows, :] = value.astype(BF16)
        return 0

    lax.fori_loop(0, n_chunks, grad_step, 0)
    for i in range(8):
        gl[:, 128 * i : 128 * (i + 1)] = glt[128 * i : 128 * (i + 1), :].T

    def term(zz, xx, cc, out):
        t = (zz * 2 + xx) * 2 + cc
        value = jnp.dot(gl[...], w[:, columns(t, 256)], preferred_element_type=F32)
        value = value.astype(out.dtype)
        out[xx, :, :, 0:64] = value[:, 0:128].reshape(2, 4, 64, 128)
        out[xx, :, :, 64:128] = value[:, 128:256].reshape(2, 4, 64, 128)

    def both(zz, cc, out):
        def step(xx, _):
            term(zz, xx, cc, out)
            return 0

        lax.fori_loop(0, 2, step, 0)

    def swap(i, s):
        both((z + s) % 4, 1 - c, give.at[i])
        return send(give.at[i], take.at[i], partner)

    slots0, slots1 = (a0, b0, c0), (a1, b1, c1)
    finals = (fa, fb, fc)
    red0, red1 = {}, {}

    def reduce_z(s):
        if s:
            ref = r.at[region(spot(0, first="all", second="all", last=s), ROWS[0])]
            red0[0, s] = send(ref, a0.at[s - 1], there({Z: s}))
        for k in (1, 2):
            for d in NEAR:
                ref = r.at[region(spot(k, first="all", second=s, last=d), ROWS[k])]
                red0[k, s, d] = send(ref, slots0[k].at[s, d - 1], there({ORDERS[k][2]: d}))

    def line(k, s):
        ix = region(spot(k, first="all", second=s), ROWS[k])
        value = r[ix].astype(F32)
        for d in NEAR:
            if k == 0:
                value = value + a0[d - 1, :, (y + s) % 4].astype(F32)
            else:
                red0[k, s, d].wait_recv()
                value = value + slots0[k][s, d - 1].astype(F32)
        return ix, value

    def pass_line(k, s):
        ix, value = line(k, s)
        r[ix] = value.astype(BF16)
        if s == 0:
            finals[k][...] = value
        for d in NEAR + (0,):
            if s or d:
                ref = r.at[region(spot(k, first=d, second=s), ROWS[k])]
                to = there({ORDERS[k][0]: d, ORDERS[k][1]: s})
                red1[k, s, d] = send(ref, slots1[k].at[s * 4 + d], to)

    def weight_grad(start, stop):
        def step(i, _):
            for h in range(2):
                rows = slice(512 * h, 512 * (h + 1))
                gw_ref[rows, columns(i, 1024)] = jnp.dot(
                    glt[rows, :], features(i), preferred_element_type=F32
                ).astype(BF16)
            return 0

        lax.fori_loop(start, stop, step, 0)

    turns = NEAR + (0,)
    swaps = [swap(0, turns[0])]
    for i, s in enumerate(turns):
        if i < 3:
            swaps.append(swap(i + 1, turns[i + 1]))
        both((z + s) % 4, c, own)
        swaps[i].wait_recv()
        for xx in range(2):
            r[:, :, (z + s) % 4, xx] = (own[xx] + take[i, xx].astype(F32)).astype(BF16)
        reduce_z(s)
    weight_grad(0, 1)
    for k in (1, 2):
        pass_line(k, 1)
    weight_grad(1, 2)
    for k in (1, 2):
        pass_line(k, 3)
    weight_grad(2, 3)
    for d in NEAR:
        red0[0, d].wait_recv()
    for s in NEAR:
        pass_line(0, s)
    pass_line(0, 0)
    for k in (1, 2):
        pass_line(k, 2)
    for k in (1, 2):
        pass_line(k, 0)
    weight_grad(3, 4)
    mine = region(me)
    for k in range(3):
        axis = ORDERS[k][0]
        n = me[axis]
        value = finals[k][(n % 2, n // 2) if axis == X else (n,)]
        for (kk, s, d), cp in red1.items():
            if kk == k:
                cp.wait_recv()
                value = value + slots1[k][s * 4 + d].astype(F32)
        r[region(me, ROWS[k])] = value.astype(BF16)
    gh_ref[:, 0:128] = r[mine + (pl.ds(0, 64),)]
    gh_ref[:, 128:256] = r[mine + (pl.ds(64, 64),)]

    assert len(copies) == COPIES, len(copies)
    for cp in copies:
        cp.wait_send()


def write_kernel(gw, loss, gh, gw_out, loss_out, gh_out, sem):
    step = gw.shape[0] // PIECES
    pairs = [(gw.at[pl.ds(i * step, step)], gw_out.at[pl.ds(i * step, step)]) for i in range(PIECES)]
    pairs += [(loss, loss_out), (gh, gh_out)]
    copies = [pltpu.make_async_copy(a, b, sem.at[i]) for i, (a, b) in enumerate(pairs)]
    for cp in copies:
        cp.start()
    for cp in copies:
        cp.wait()


def shards(hidden, weight, targets, loss_grad):
    vocab, depth = weight.shape
    tokens = targets.shape[0]
    dma = pltpu.SemaphoreType.DMA
    vmem = pl.BlockSpec(memory_space=pltpu.VMEM)
    anywhere = pl.BlockSpec(memory_space=pl.ANY)
    slot = lambda *s, t=BF16: pltpu.VMEM(s + (128,), t)
    loss, grad_hidden, grad_weight = pl.pallas_call(
        kernel,
        out_shape=(
            pltpu.VMEM((4, 128), F32),
            pltpu.VMEM(hidden.shape, BF16),
            pltpu.VMEM((vocab, depth), BF16),
        ),
        in_specs=[vmem, anywhere, vmem, vmem],
        out_specs=(vmem, vmem, vmem),
        scratch_shapes=[
            pltpu.VMEM((vocab, depth), BF16),
            pltpu.VMEM((2, 2, 4, 4, 2, 128, 128), BF16),
            pltpu.VMEM((vocab, tokens), F32),
            pltpu.VMEM((vocab, tokens), BF16),
            pltpu.VMEM((tokens, vocab), BF16),
            pltpu.VMEM((2, 2, 4, 128, 128), F32),
            pltpu.VMEM((4, 2, 2, 4, 128, 128), BF16),
            pltpu.VMEM((4, 2, 2, 4, 128, 128), BF16),
            pltpu.VMEM((2, 4, 4, 2, 128, 128), BF16),
            slot(3, 2, 4, 2, 32), slot(4, 3, 4, 48), slot(4, 3, 2, 2, 48),
            slot(16, 32), slot(16, 48), slot(16, 48),
            slot(2, 2, 32, t=F32), slot(4, 48, t=F32), slot(2, 2, 48, t=F32),
            pltpu.VMEM((16, 3, 4, 128), F32),
            pltpu.VMEM((8, 3, 4, 128), F32),
            dma, dma((COPIES,)), dma((COPIES,)),
        ],
        compiler_params=pltpu.CompilerParams(
            collective_id=0, has_side_effects=True, vmem_limit_bytes=48 * 2**20
        ),
    )(hidden, weight, targets.reshape(1, tokens), loss_grad.reshape(1, tokens))
    grad_weight, loss, grad_hidden = pl.pallas_call(
        write_kernel,
        out_shape=(
            jax.ShapeDtypeStruct((vocab, depth), BF16),
            jax.ShapeDtypeStruct((4, 128), F32),
            jax.ShapeDtypeStruct(hidden.shape, BF16),
        ),
        in_specs=[vmem] * 3,
        out_specs=(anywhere,) * 3,
        scratch_shapes=[dma((PIECES + 2,))],
        compiler_params=pltpu.CompilerParams(vmem_limit_bytes=16 * 2**20),
    )(grad_weight, loss, grad_hidden)
    return loss.reshape(tokens), grad_hidden, grad_weight


def solution(mesh):
    return jax.shard_map(
        shards,
        mesh=mesh,
        in_specs=(P("section", "tensor"), P(("section", "tensor"), None), P(), P()),
        out_specs=(P(), P("section", "tensor"), P(("section", "tensor"), None)),
        check_vma=False,
    )
```

```python
import jax
import jax.numpy as jnp
from jax import lax
from jax.experimental import pallas as pl
from jax.experimental.pallas import tpu as pltpu
from jax.sharding import PartitionSpec as P

MESH = pl.DeviceIdType.MESH
F32, BF16 = jnp.float32, jnp.bfloat16
X, Y, Z = 0, 1, 2

ORDERS = ((X, Y, Z), (Y, Z, X), (X, Z, Y))
ROWS = ((0, 32), (32, 48), (80, 48))
NEAR = (1, 3, 2)
COPIES = 188
PIECES = 8


def place():
    s, t = lax.axis_index("section"), lax.axis_index("tensor")
    return ((t // 2) % 2) * 2 + s // 4, s % 4, t // 4, t % 2


def device(x, y, z, c):
    return ((x % 2) * 4 + y, z * 4 + (x // 2) * 2 + c)


def region(at, rows=None):
    x, y, z = at
    whole = slice(None)
    ix = (
        whole if x is None else x % 2,
        whole if y is None else y,
        whole if z is None else z,
        whole if x is None else x // 2,
    )
    return ix if rows is None else ix + (pl.ds(rows[0], rows[1]),)


def combine(parts):
    top = jnp.max(parts[:, 0], axis=0)
    total = jnp.sum(parts[:, 1] * jnp.exp(parts[:, 0] - top[None]), axis=0)
    return top, total, jnp.sum(parts[:, 2], axis=0)


def flat(rows):
    return jnp.concatenate([rows[i : i + 1] for i in range(4)], axis=1)


def kernel(
    hid_hbm, w_hbm, tgt_hbm, lg_hbm,
    loss_ref, gh_ref, gw_ref,
    w, g, lt, glt, gl, own, give, take, r,
    a0, b0, c0, a1, b1, c1, fa, fb, fc,
    st_core, st_plane, st_axis,
    tgt_ref, lg_ref, local_sem, send_sem, recv_sem,
):
    x, y, z, c = place()
    me = (x, y, z)
    vocab, depth = w.shape
    tokens = lt.shape[1]
    partner = device(x, y, z, 1 - c)

    def settle(upto=None):
        upto = len(copies) if upto is None else upto
        for cp in copies[len(settled) : upto]:
            cp.wait_send()
            settled.append(cp)

    def there(moves):
        return device(*[(me[a] + moves.get(a, 0)) % 4 for a in range(3)], c)

    barrier = pltpu.get_barrier_semaphore()
    peers = [partner]
    for d in NEAR:
        peers += [there({axis: d}) for axis in (X, Y, Z)]
        peers += [there({p: d, q: e}) for p, q in ((X, Y), (Y, Z), (X, Z)) for e in NEAR]
    for to in peers:
        pl.semaphore_signal(barrier, inc=1, device_id=to, device_id_type=MESH)
    own_g = (c,) + region(me)
    pairs = [
        (hid_hbm.at[:, pl.ds(0, 128)], g.at[own_g + (pl.ds(0, 64),)]),
        (hid_hbm.at[:, pl.ds(128, 128)], g.at[own_g + (pl.ds(64, 64),)]),
        (tgt_hbm, tgt_ref), (lg_hbm, lg_ref), (w_hbm, w),
    ]
    loads = [pltpu.make_async_copy(a, b, local_sem.at[i]) for i, (a, b) in enumerate(pairs)]
    for cp in loads:
        cp.start()
    lt[...] = jnp.zeros_like(lt)
    for cp in loads[:4]:
        cp.wait()
    pl.semaphore_wait(barrier, len(peers))

    copies, settled = [], []

    def send(src, dst, to):
        i = len(copies)
        cp = pltpu.make_async_remote_copy(
            src, dst, send_sem.at[i], recv_sem.at[i], device_id=to, device_id_type=MESH
        )
        cp.start()
        copies.append(cp)
        return cp

    def spot(k, **at):
        out = [None, None, None]
        for name, axis in zip(("first", "second", "last"), ORDERS[k]):
            d = at.get(name, 0)
            out[axis] = None if d == "all" else (me[axis] + d) % 4
        return tuple(out)

    def spread(k, to, **at):
        ref = g.at[(c,) + region(spot(k, **at), ROWS[k])]
        return send(ref, ref, to)

    got1, got2 = {}, {}
    for s in (0,) + NEAR:
        for k in range(3):
            for d in (0,) + NEAR:
                if s or d:
                    got1[k, s, d] = spread(k, there({ORDERS[k][0]: d, ORDERS[k][1]: s}))
    for s in (0,) + NEAR:
        for k in range(3):
            for d in (0,) + NEAR:
                if s or d:
                    got1[k, s, d].wait_recv()
            for d in NEAR:
                got2[k, s, d] = spread(k, there({ORDERS[k][2]: d}), first="all", second=-s)

    def relay(s):
        done = []
        for k in range(3):
            if k == 0:
                if s:
                    for i in (0,) + NEAR:
                        got2[0, i, s].wait_recv()
            else:
                for d in NEAR:
                    got2[k, s, d].wait_recv()
            ref = g.at[(c,) + region((None, None, (z - s) % 4), ROWS[k])]
            done.append(send(ref, ref, partner))
        return done

    def features(zz, classes=(0, 1)):
        parts = [
            g[cc, :, :, zz, xx, pl.ds(64 * h, 64), :].reshape(tokens, 128)
            for xx in range(2)
            for cc in classes
            for h in range(2)
        ]
        return jnp.concatenate(parts, axis=1)

    def columns(i, width):
        return pl.ds(pl.multiple_of(i * width, width), width)

    def logits(s, cc=None):
        zz = (z - s) % 4
        if cc is None:
            part, rhs = w[:, columns(zz, 1024)], features(zz)
        else:
            part = jnp.concatenate([w[:, columns((zz * 2 + xx) * 2 + cc, 256)] for xx in range(2)], axis=1)
            rhs = features(zz, (cc,))
        lt[...] += lax.dot_general(
            part, rhs, (((1,), (1,)), ((), ())), preferred_element_type=F32
        )

    def arrived(relayed):
        for cp in relayed:
            cp.wait_recv()

    relayed = {0: relay(0)}
    loads[4].wait()
    arrived(relayed[0])
    logits(0)
    for s in NEAR:
        relayed[s] = relay(s)
    logits(1, c)
    arrived(relayed[1])
    logits(1, 1 - c)
    arrived(relayed[3])
    logits(3)
    arrived(relayed[2])
    logits(2)

    s_idx, t_idx = lax.axis_index("section"), lax.axis_index("tensor")
    local = tgt_ref[...] - (s_idx * 16 + t_idx) * vocab
    chunk = 64
    n_chunks = vocab // chunk

    def hit(i):
        ids = lax.broadcasted_iota(jnp.int32, (chunk, tokens), 0) + i * chunk
        return ids == local

    def max_step(i, top):
        return jnp.maximum(top, lt[pl.ds(pl.multiple_of(i * chunk, chunk), chunk), :])

    top = lax.fori_loop(1, n_chunks, max_step, lt[pl.ds(0, chunk), :])
    top = jnp.max(top, axis=0, keepdims=True)

    def exp_step(i, carry):
        total, picked = carry
        rows = pl.ds(pl.multiple_of(i * chunk, chunk), chunk)
        value = lt[rows, :]
        e = jnp.exp(value - top)
        lt[rows, :] = e
        picked = picked + jnp.sum(jnp.where(hit(i), value, 0.0), axis=0, keepdims=True)
        return total + jnp.sum(e, axis=0, keepdims=True), picked

    zero = jnp.zeros((1, tokens), F32)
    total, picked = lax.fori_loop(0, n_chunks, exp_step, (zero, zero))

    for j, v in enumerate((top, total, picked)):
        for i in range(4):
            st_core[0, j, i : i + 1, :] = v[:, 128 * i : 128 * (i + 1)]
    gathered = len(copies)
    send(st_core.at[0], st_core.at[1], partner).wait_recv()
    for j, v in enumerate(combine(st_core[...])):
        st_plane[0, j] = v
    joined = []
    for dx in range(4):
        for dy in range(4):
            i = dx * 4 + dy
            if i:
                joined.append(send(st_plane.at[0], st_plane.at[i], there({X: dx, Y: dy})))
    settle(gathered)
    for cp in joined:
        cp.wait_recv()
    for j, v in enumerate(combine(st_plane[...])):
        st_axis[0, j] = v
    joined = [send(st_axis.at[0], st_axis.at[d], there({Z: d})) for d in NEAR]
    settle(len(copies) - len(joined))
    for cp in joined:
        cp.wait_recv()
    m_all, s_all, p_all = combine(st_axis[...])
    loss_ref[...] = m_all + jnp.log(s_all) - p_all
    lg = lg_ref[...]
    scale = lg * jnp.exp(top - flat(m_all)) / flat(s_all)

    def grad_step(i, _):
        rows = pl.ds(pl.multiple_of(i * chunk, chunk), chunk)
        value = lt[rows, :] * scale - jnp.where(hit(i), lg, 0.0)
        glt[rows, :] = value.astype(BF16)
        return 0

    lax.fori_loop(0, n_chunks, grad_step, 0)
    for i in range(8):
        gl[:, 128 * i : 128 * (i + 1)] = glt[128 * i : 128 * (i + 1), :].T

    def term(zz, xx, cc, out):
        t = (zz * 2 + xx) * 2 + cc
        value = jnp.dot(gl[...], w[:, columns(t, 256)], preferred_element_type=F32)
        value = value.astype(out.dtype)
        out[xx, :, :, 0:64] = value[:, 0:128].reshape(2, 4, 64, 128)
        out[xx, :, :, 64:128] = value[:, 128:256].reshape(2, 4, 64, 128)

    def both(zz, cc, out):
        def step(xx, _):
            term(zz, xx, cc, out)
            return 0

        lax.fori_loop(0, 2, step, 0)

    def swap(i, s):
        both((z + s) % 4, 1 - c, give.at[i])
        return send(give.at[i], take.at[i], partner)

    slots0, slots1 = (a0, b0, c0), (a1, b1, c1)
    finals = (fa, fb, fc)
    red0, red1 = {}, {}

    def reduce_z(s):
        if s:
            ref = r.at[region(spot(0, first="all", second="all", last=s), ROWS[0])]
            red0[0, s] = send(ref, a0.at[s - 1], there({Z: s}))
        for k in (1, 2):
            for d in NEAR:
                ref = r.at[region(spot(k, first="all", second=s, last=d), ROWS[k])]
                red0[k, s, d] = send(ref, slots0[k].at[s, d - 1], there({ORDERS[k][2]: d}))

    def line(k, s):
        ix = region(spot(k, first="all", second=s), ROWS[k])
        value = r[ix].astype(F32)
        for d in NEAR:
            if k == 0:
                value = value + a0[d - 1, :, (y + s) % 4].astype(F32)
            else:
                red0[k, s, d].wait_recv()
                value = value + slots0[k][s, d - 1].astype(F32)
        return ix, value

    def pass_line(k, s):
        ix, value = line(k, s)
        r[ix] = value.astype(BF16)
        if s == 0:
            finals[k][...] = value
        for d in NEAR + (0,):
            if s or d:
                ref = r.at[region(spot(k, first=d, second=s), ROWS[k])]
                to = there({ORDERS[k][0]: d, ORDERS[k][1]: s})
                red1[k, s, d] = send(ref, slots1[k].at[s * 4 + d], to)

    def weight_grad(start, stop):
        def step(i, _):
            for h in range(2):
                rows = slice(512 * h, 512 * (h + 1))
                gw_ref[rows, columns(i, 1024)] = jnp.dot(
                    glt[rows, :], features(i), preferred_element_type=F32
                ).astype(BF16)
            return 0

        lax.fori_loop(start, stop, step, 0)

    turns = NEAR + (0,)
    swaps = [swap(0, turns[0])]
    for i, s in enumerate(turns):
        if i < 3:
            swaps.append(swap(i + 1, turns[i + 1]))
        both((z + s) % 4, c, own)
        swaps[i].wait_recv()
        for xx in range(2):
            r[:, :, (z + s) % 4, xx] = (own[xx] + take[i, xx].astype(F32)).astype(BF16)
        reduce_z(s)
    weight_grad(0, 1)
    reduced = len(copies)
    for k in (1, 2):
        pass_line(k, 1)
    weight_grad(1, 2)
    for k in (1, 2):
        pass_line(k, 3)
    weight_grad(2, 3)
    for d in NEAR:
        red0[0, d].wait_recv()
    for s in NEAR:
        pass_line(0, s)
    pass_line(0, 0)
    for k in (1, 2):
        pass_line(k, 2)
    for k in (1, 2):
        pass_line(k, 0)
    weight_grad(3, 4)
    settle(reduced)
    mine = region(me)
    for k in range(3):
        axis = ORDERS[k][0]
        n = me[axis]
        value = finals[k][(n % 2, n // 2) if axis == X else (n,)]
        for (kk, s, d), cp in red1.items():
            if kk == k:
                cp.wait_recv()
                value = value + slots1[k][s * 4 + d].astype(F32)
        r[region(me, ROWS[k])] = value.astype(BF16)
    gh_ref[:, 0:128] = r[mine + (pl.ds(0, 64),)]
    gh_ref[:, 128:256] = r[mine + (pl.ds(64, 64),)]

    assert len(copies) == COPIES, len(copies)
    settle()


def write_kernel(gw, loss, gh, gw_out, loss_out, gh_out, sem):
    step = gw.shape[0] // PIECES
    pairs = [(gw.at[pl.ds(i * step, step)], gw_out.at[pl.ds(i * step, step)]) for i in range(PIECES)]
    pairs += [(loss, loss_out), (gh, gh_out)]
    copies = [pltpu.make_async_copy(a, b, sem.at[i]) for i, (a, b) in enumerate(pairs)]
    for cp in copies:
        cp.start()
    for cp in copies:
        cp.wait()


def shards(hidden, weight, targets, loss_grad):
    vocab, depth = weight.shape
    tokens = targets.shape[0]
    dma = pltpu.SemaphoreType.DMA
    vmem = pl.BlockSpec(memory_space=pltpu.VMEM)
    anywhere = pl.BlockSpec(memory_space=pl.ANY)
    slot = lambda *s, t=BF16: pltpu.VMEM(s + (128,), t)
    loss, grad_hidden, grad_weight = pl.pallas_call(
        kernel,
        out_shape=(
            pltpu.VMEM((4, 128), F32),
            pltpu.VMEM(hidden.shape, BF16),
            pltpu.VMEM((vocab, depth), BF16),
        ),
        in_specs=[anywhere] * 4,
        out_specs=(vmem, vmem, vmem),
        scratch_shapes=[
            pltpu.VMEM((vocab, depth), BF16),
            pltpu.VMEM((2, 2, 4, 4, 2, 128, 128), BF16),
            pltpu.VMEM((vocab, tokens), F32),
            pltpu.VMEM((vocab, tokens), BF16),
            pltpu.VMEM((tokens, vocab), BF16),
            pltpu.VMEM((2, 2, 4, 128, 128), F32),
            pltpu.VMEM((4, 2, 2, 4, 128, 128), BF16),
            pltpu.VMEM((4, 2, 2, 4, 128, 128), BF16),
            pltpu.VMEM((2, 4, 4, 2, 128, 128), BF16),
            slot(3, 2, 4, 2, 32), slot(4, 3, 4, 48), slot(4, 3, 2, 2, 48),
            slot(16, 32), slot(16, 48), slot(16, 48),
            slot(2, 2, 32, t=F32), slot(4, 48, t=F32), slot(2, 2, 48, t=F32),
            pltpu.VMEM((2, 3, 4, 128), F32),
            pltpu.VMEM((16, 3, 4, 128), F32),
            pltpu.VMEM((4, 3, 4, 128), F32),
            pltpu.VMEM((1, tokens), jnp.int32),
            pltpu.VMEM((1, tokens), F32),
            dma((5,)), dma((COPIES,)), dma((COPIES,)),
        ],
        compiler_params=pltpu.CompilerParams(
            collective_id=0, has_side_effects=True, vmem_limit_bytes=48 * 2**20
        ),
    )(hidden, weight, targets.reshape(1, tokens), loss_grad.reshape(1, tokens))
    grad_weight, loss, grad_hidden = pl.pallas_call(
        write_kernel,
        out_shape=(
            jax.ShapeDtypeStruct((vocab, depth), BF16),
            jax.ShapeDtypeStruct((4, 128), F32),
            jax.ShapeDtypeStruct(hidden.shape, BF16),
        ),
        in_specs=[vmem] * 3,
        out_specs=(anywhere,) * 3,
        scratch_shapes=[dma((PIECES + 2,))],
        compiler_params=pltpu.CompilerParams(vmem_limit_bytes=16 * 2**20),
    )(grad_weight, loss, grad_hidden)
    return loss.reshape(tokens), grad_hidden, grad_weight


def solution(mesh):
    return jax.shard_map(
        shards,
        mesh=mesh,
        in_specs=(P("section", "tensor"), P(("section", "tensor"), None), P(), P()),
        out_specs=(P(), P("section", "tensor"), P(("section", "tensor"), None)),
        check_vma=False,
    )
```

```python
import jax
import jax.numpy as jnp
from jax import lax
from jax.experimental import pallas as pl
from jax.experimental.pallas import tpu as pltpu
from jax.sharding import PartitionSpec as P

MESH = pl.DeviceIdType.MESH
F32, BF16 = jnp.float32, jnp.bfloat16
X, Y, Z = 0, 1, 2

ORDERS = ((X, Y, Z), (Y, Z, X), (X, Z, Y))
ROWS = ((0, 32), (32, 48), (80, 48))
NEAR = (1, 3, 2)
COPIES = 185
PIECES = 8


def place():
    s, t = lax.axis_index("section"), lax.axis_index("tensor")
    return ((t // 2) % 2) * 2 + s // 4, s % 4, t // 4, t % 2


def device(x, y, z, c):
    return ((x % 2) * 4 + y, z * 4 + (x // 2) * 2 + c)


def region(at, rows=None):
    x, y, z = at
    whole = slice(None)
    ix = (
        whole if x is None else x % 2,
        whole if y is None else y,
        whole if z is None else z,
        whole if x is None else x // 2,
    )
    return ix if rows is None else ix + (pl.ds(rows[0], rows[1]),)


def combine(parts):
    top = jnp.max(parts[:, 0], axis=0)
    total = jnp.sum(parts[:, 1] * jnp.exp(parts[:, 0] - top[None]), axis=0)
    return top, total, jnp.sum(parts[:, 2], axis=0)


def flat(rows):
    return jnp.concatenate([rows[i : i + 1] for i in range(4)], axis=1)


def kernel(
    hid_hbm, w_hbm, tgt_hbm, lg_hbm,
    loss_ref, gh_ref, gw_ref,
    w, g, lt, glt, gl, own, give, take, r,
    a0, b0, c0, a1, b1, c1, fa, fb, fc,
    st_core, st_plane, st_axis,
    tgt_ref, lg_ref, local_sem, send_sem, recv_sem,
):
    x, y, z, c = place()
    me = (x, y, z)
    vocab, depth = w.shape
    tokens = lt.shape[1]
    partner = device(x, y, z, 1 - c)

    def settle(upto=None):
        upto = len(copies) if upto is None else upto
        for cp in copies[len(settled) : upto]:
            cp.wait_send()
            settled.append(cp)

    def there(moves):
        return device(*[(me[a] + moves.get(a, 0)) % 4 for a in range(3)], c)

    barrier = pltpu.get_barrier_semaphore()
    peers = [partner]
    for d in NEAR:
        peers += [there({axis: d}) for axis in (X, Y, Z)]
        peers += [there({p: d, q: e}) for p, q in ((X, Y), (Y, Z), (X, Z)) for e in NEAR]
    for to in peers:
        pl.semaphore_signal(barrier, inc=1, device_id=to, device_id_type=MESH)
    own_g = (c,) + region(me)
    pairs = [
        (hid_hbm.at[:, pl.ds(0, 128)], g.at[own_g + (pl.ds(0, 64),)]),
        (hid_hbm.at[:, pl.ds(128, 128)], g.at[own_g + (pl.ds(64, 64),)]),
        (tgt_hbm, tgt_ref), (lg_hbm, lg_ref), (w_hbm, w),
    ]
    loads = [pltpu.make_async_copy(a, b, local_sem.at[i]) for i, (a, b) in enumerate(pairs)]
    for cp in loads:
        cp.start()
    lt[...] = jnp.zeros_like(lt)
    for cp in loads[:4]:
        cp.wait()
    pl.semaphore_wait(barrier, len(peers))

    copies, settled = [], []

    def send(src, dst, to):
        i = len(copies)
        cp = pltpu.make_async_remote_copy(
            src, dst, send_sem.at[i], recv_sem.at[i], device_id=to, device_id_type=MESH
        )
        cp.start()
        copies.append(cp)
        return cp

    def spot(k, **at):
        out = [None, None, None]
        for name, axis in zip(("first", "second", "last"), ORDERS[k]):
            d = at.get(name, 0)
            out[axis] = None if d == "all" else (me[axis] + d) % 4
        return tuple(out)

    def spread(k, to, **at):
        ref = g.at[(c,) + region(spot(k, **at), ROWS[k])]
        return send(ref, ref, to)

    got1, got2 = {}, {}
    for s in (0,) + NEAR:
        for k in range(3):
            for d in (0,) + NEAR:
                if s or d:
                    got1[k, s, d] = spread(k, there({ORDERS[k][0]: d, ORDERS[k][1]: s}))
    for s in (0,) + NEAR:
        for k in range(3):
            for d in (0,) + NEAR:
                if s or d:
                    got1[k, s, d].wait_recv()
            for d in NEAR if k else (1, 3):
                got2[k, s, d] = spread(k, there({ORDERS[k][2]: d}), first="all", second=-s)
    got2[0, 0, 2] = spread(0, there({Z: 2}), first="all", second="all")

    def relay(s):
        done = []
        for k in range(3):
            if k == 0:
                if s:
                    for i in (0,) if s == 2 else (0,) + NEAR:
                        got2[0, i, s].wait_recv()
            else:
                for d in NEAR:
                    got2[k, s, d].wait_recv()
            ref = g.at[(c,) + region((None, None, (z - s) % 4), ROWS[k])]
            done.append(send(ref, ref, partner))
        return done

    def features(zz, classes=(0, 1)):
        parts = [
            g[cc, :, :, zz, xx, pl.ds(64 * h, 64), :].reshape(tokens, 128)
            for xx in range(2)
            for cc in classes
            for h in range(2)
        ]
        return jnp.concatenate(parts, axis=1)

    def columns(i, width):
        return pl.ds(pl.multiple_of(i * width, width), width)

    def logits(s, cc=None):
        zz = (z - s) % 4
        if cc is None:
            part, rhs = w[:, columns(zz, 1024)], features(zz)
        else:
            part = jnp.concatenate([w[:, columns((zz * 2 + xx) * 2 + cc, 256)] for xx in range(2)], axis=1)
            rhs = features(zz, (cc,))
        lt[...] += lax.dot_general(
            part, rhs, (((1,), (1,)), ((), ())), preferred_element_type=F32
        )

    def arrived(relayed):
        for cp in relayed:
            cp.wait_recv()

    relayed = {0: relay(0)}
    loads[4].wait()
    arrived(relayed[0])
    logits(0)
    for s in NEAR:
        relayed[s] = relay(s)
    logits(1, c)
    arrived(relayed[1])
    logits(1, 1 - c)
    arrived(relayed[3])
    logits(3)
    arrived(relayed[2])
    logits(2)

    s_idx, t_idx = lax.axis_index("section"), lax.axis_index("tensor")
    local = tgt_ref[...] - (s_idx * 16 + t_idx) * vocab
    chunk = 64
    n_chunks = vocab // chunk

    def hit(i):
        ids = lax.broadcasted_iota(jnp.int32, (chunk, tokens), 0) + i * chunk
        return ids == local

    def max_step(i, top):
        return jnp.maximum(top, lt[pl.ds(pl.multiple_of(i * chunk, chunk), chunk), :])

    top = lax.fori_loop(1, n_chunks, max_step, lt[pl.ds(0, chunk), :])
    top = jnp.max(top, axis=0, keepdims=True)

    def exp_step(i, carry):
        total, picked = carry
        rows = pl.ds(pl.multiple_of(i * chunk, chunk), chunk)
        value = lt[rows, :]
        e = jnp.exp(value - top)
        lt[rows, :] = e
        picked = picked + jnp.sum(jnp.where(hit(i), value, 0.0), axis=0, keepdims=True)
        return total + jnp.sum(e, axis=0, keepdims=True), picked

    zero = jnp.zeros((1, tokens), F32)
    total, picked = lax.fori_loop(0, n_chunks, exp_step, (zero, zero))

    for j, v in enumerate((top, total, picked)):
        for i in range(4):
            st_core[0, j, i : i + 1, :] = v[:, 128 * i : 128 * (i + 1)]
    gathered = len(copies)
    send(st_core.at[0], st_core.at[1], partner).wait_recv()
    for j, v in enumerate(combine(st_core[...])):
        st_plane[0, j] = v
    joined = []
    for dx in range(4):
        for dy in range(4):
            i = dx * 4 + dy
            if i:
                joined.append(send(st_plane.at[0], st_plane.at[i], there({X: dx, Y: dy})))
    settle(gathered)
    for cp in joined:
        cp.wait_recv()
    for j, v in enumerate(combine(st_plane[...])):
        st_axis[0, j] = v
    joined = [send(st_axis.at[0], st_axis.at[d], there({Z: d})) for d in NEAR]
    settle(len(copies) - len(joined))
    for cp in joined:
        cp.wait_recv()
    m_all, s_all, p_all = combine(st_axis[...])
    loss_ref[...] = m_all + jnp.log(s_all) - p_all
    lg = lg_ref[...]
    scale = jnp.exp(top - flat(m_all)) / flat(s_all)

    def grad_step(i, _):
        rows = pl.ds(pl.multiple_of(i * chunk, chunk), chunk)
        value = lg * (lt[rows, :] * scale - jnp.where(hit(i), 1.0, 0.0))
        glt[rows, :] = value.astype(BF16)
        return 0

    lax.fori_loop(0, n_chunks, grad_step, 0)
    for i in range(8):
        gl[:, 128 * i : 128 * (i + 1)] = glt[128 * i : 128 * (i + 1), :].T

    def term(zz, xx, cc, out):
        t = (zz * 2 + xx) * 2 + cc
        value = jnp.dot(gl[...], w[:, columns(t, 256)], preferred_element_type=F32)
        value = value.astype(out.dtype)
        out[xx, :, :, 0:64] = value[:, 0:128].reshape(2, 4, 64, 128)
        out[xx, :, :, 64:128] = value[:, 128:256].reshape(2, 4, 64, 128)

    def both(zz, cc, out):
        def step(xx, _):
            term(zz, xx, cc, out)
            return 0

        lax.fori_loop(0, 2, step, 0)

    def swap(i, s):
        both((z + s) % 4, 1 - c, give.at[i])
        return send(give.at[i], take.at[i], partner)

    slots0, slots1 = (a0, b0, c0), (a1, b1, c1)
    finals = (fa, fb, fc)
    red0, red1 = {}, {}

    def reduce_z(s):
        if s:
            ref = r.at[region(spot(0, first="all", second="all", last=s), ROWS[0])]
            red0[0, s] = send(ref, a0.at[s - 1], there({Z: s}))
        for k in (1, 2):
            for d in NEAR:
                ref = r.at[region(spot(k, first="all", second=s, last=d), ROWS[k])]
                red0[k, s, d] = send(ref, slots0[k].at[s, d - 1], there({ORDERS[k][2]: d}))

    def line(k, s):
        ix = region(spot(k, first="all", second=s), ROWS[k])
        value = r[ix].astype(F32)
        for d in NEAR:
            if k == 0:
                value = value + a0[d - 1, :, (y + s) % 4].astype(F32)
            else:
                red0[k, s, d].wait_recv()
                value = value + slots0[k][s, d - 1].astype(F32)
        return ix, value

    def pass_line(k, s):
        ix, value = line(k, s)
        r[ix] = value.astype(BF16)
        if s == 0:
            finals[k][...] = value
        for d in NEAR + (0,):
            if s or d:
                ref = r.at[region(spot(k, first=d, second=s), ROWS[k])]
                to = there({ORDERS[k][0]: d, ORDERS[k][1]: s})
                red1[k, s, d] = send(ref, slots1[k].at[s * 4 + d], to)

    def weight_grad(start, stop):
        def step(i, _):
            for h in range(2):
                rows = slice(512 * h, 512 * (h + 1))
                gw_ref[rows, columns(i, 1024)] = jnp.dot(
                    glt[rows, :], features(i), preferred_element_type=F32
                ).astype(BF16)
            return 0

        lax.fori_loop(start, stop, step, 0)

    turns = NEAR + (0,)
    swaps = [swap(0, turns[0])]
    for i, s in enumerate(turns):
        if i < 3:
            swaps.append(swap(i + 1, turns[i + 1]))
        both((z + s) % 4, c, own)
        swaps[i].wait_recv()
        for xx in range(2):
            r[:, :, (z + s) % 4, xx] = (own[xx] + take[i, xx].astype(F32)).astype(BF16)
        reduce_z(s)
    weight_grad(0, 1)
    reduced = len(copies)
    for k in (1, 2):
        pass_line(k, 1)
    weight_grad(1, 2)
    for k in (1, 2):
        pass_line(k, 3)
    weight_grad(2, 3)
    for d in NEAR:
        red0[0, d].wait_recv()
    for s in NEAR:
        pass_line(0, s)
    pass_line(0, 0)
    for k in (1, 2):
        pass_line(k, 2)
    for k in (1, 2):
        pass_line(k, 0)
    weight_grad(3, 4)
    settle(reduced)
    mine = region(me)
    for k in range(3):
        axis = ORDERS[k][0]
        n = me[axis]
        value = finals[k][(n % 2, n // 2) if axis == X else (n,)]
        for (kk, s, d), cp in red1.items():
            if kk == k:
                cp.wait_recv()
                value = value + slots1[k][s * 4 + d].astype(F32)
        r[region(me, ROWS[k])] = value.astype(BF16)
    gh_ref[:, 0:128] = r[mine + (pl.ds(0, 64),)]
    gh_ref[:, 128:256] = r[mine + (pl.ds(64, 64),)]

    assert len(copies) == COPIES, len(copies)
    settle()


def write_kernel(gw, loss, gh, gw_out, loss_out, gh_out, sem):
    step = gw.shape[0] // PIECES
    pairs = [(gw.at[pl.ds(i * step, step)], gw_out.at[pl.ds(i * step, step)]) for i in range(PIECES)]
    pairs += [(loss, loss_out), (gh, gh_out)]
    copies = [pltpu.make_async_copy(a, b, sem.at[i]) for i, (a, b) in enumerate(pairs)]
    for cp in copies:
        cp.start()
    for cp in copies:
        cp.wait()


def shards(hidden, weight, targets, loss_grad):
    vocab, depth = weight.shape
    tokens = targets.shape[0]
    dma = pltpu.SemaphoreType.DMA
    vmem = pl.BlockSpec(memory_space=pltpu.VMEM)
    anywhere = pl.BlockSpec(memory_space=pl.ANY)
    slot = lambda *s, t=BF16: pltpu.VMEM(s + (128,), t)
    loss, grad_hidden, grad_weight = pl.pallas_call(
        kernel,
        out_shape=(
            pltpu.VMEM((4, 128), F32),
            pltpu.VMEM(hidden.shape, BF16),
            pltpu.VMEM((vocab, depth), BF16),
        ),
        in_specs=[anywhere] * 4,
        out_specs=(vmem, vmem, vmem),
        scratch_shapes=[
            pltpu.VMEM((vocab, depth), BF16),
            pltpu.VMEM((2, 2, 4, 4, 2, 128, 128), BF16),
            pltpu.VMEM((vocab, tokens), F32),
            pltpu.VMEM((vocab, tokens), BF16),
            pltpu.VMEM((tokens, vocab), BF16),
            pltpu.VMEM((2, 2, 4, 128, 128), F32),
            pltpu.VMEM((4, 2, 2, 4, 128, 128), BF16),
            pltpu.VMEM((4, 2, 2, 4, 128, 128), BF16),
            pltpu.VMEM((2, 4, 4, 2, 128, 128), BF16),
            slot(3, 2, 4, 2, 32), slot(4, 3, 4, 48), slot(4, 3, 2, 2, 48),
            slot(16, 32), slot(16, 48), slot(16, 48),
            slot(2, 2, 32, t=F32), slot(4, 48, t=F32), slot(2, 2, 48, t=F32),
            pltpu.VMEM((2, 3, 4, 128), F32),
            pltpu.VMEM((16, 3, 4, 128), F32),
            pltpu.VMEM((4, 3, 4, 128), F32),
            pltpu.VMEM((1, tokens), jnp.int32),
            pltpu.VMEM((1, tokens), F32),
            dma((5,)), dma((COPIES,)), dma((COPIES,)),
        ],
        compiler_params=pltpu.CompilerParams(
            collective_id=0, has_side_effects=True, vmem_limit_bytes=48 * 2**20
        ),
    )(hidden, weight, targets.reshape(1, tokens), loss_grad.reshape(1, tokens))
    grad_weight, loss, grad_hidden = pl.pallas_call(
        write_kernel,
        out_shape=(
            jax.ShapeDtypeStruct((vocab, depth), BF16),
            jax.ShapeDtypeStruct((4, 128), F32),
            jax.ShapeDtypeStruct(hidden.shape, BF16),
        ),
        in_specs=[vmem] * 3,
        out_specs=(anywhere,) * 3,
        scratch_shapes=[dma((PIECES + 2,))],
        compiler_params=pltpu.CompilerParams(vmem_limit_bytes=16 * 2**20),
    )(grad_weight, loss, grad_hidden)
    return loss.reshape(tokens), grad_hidden, grad_weight


def solution(mesh):
    return jax.shard_map(
        shards,
        mesh=mesh,
        in_specs=(P("section", "tensor"), P(("section", "tensor"), None), P(), P()),
        out_specs=(P(), P("section", "tensor"), P(("section", "tensor"), None)),
        check_vma=False,
    )
```

```python
import jax
import jax.numpy as jnp
from jax import lax
from jax.experimental import pallas as pl
from jax.experimental.pallas import tpu as pltpu
from jax.sharding import PartitionSpec as P

MESH = pl.DeviceIdType.MESH
F32, BF16 = jnp.float32, jnp.bfloat16
X, Y, Z = 0, 1, 2

ORDERS = ((X, Y, Z), (Y, Z, X), (X, Z, Y))
ROWS = ((0, 32), (32, 48), (80, 48))
NEAR = (1, 3, 2)
COPIES = 188
PIECES = 8


def place():
    s, t = lax.axis_index("section"), lax.axis_index("tensor")
    return ((t // 2) % 2) * 2 + s // 4, s % 4, t // 4, t % 2


def device(x, y, z, c):
    return ((x % 2) * 4 + y, z * 4 + (x // 2) * 2 + c)


def region(at, rows=None):
    x, y, z = at
    whole = slice(None)
    ix = (
        whole if x is None else x % 2,
        whole if y is None else y,
        whole if z is None else z,
        whole if x is None else x // 2,
    )
    return ix if rows is None else ix + (pl.ds(rows[0], rows[1]),)


def combine(parts):
    top = jnp.max(parts[:, 0], axis=0)
    total = jnp.sum(parts[:, 1] * jnp.exp(parts[:, 0] - top[None]), axis=0)
    return top, total, jnp.sum(parts[:, 2], axis=0)


def flat(rows):
    return jnp.concatenate([rows[i : i + 1] for i in range(4)], axis=1)


def kernel(
    hid_hbm, w_hbm, tgt_hbm, lg_hbm,
    loss_ref, gh_ref, gw_ref,
    w, g, lt, glt, gl, own, give, take, r,
    a0, b0, c0, a1, b1, c1, fa, fb, fc,
    st_core, st_plane, st_axis,
    tgt_ref, lg_ref, local_sem, send_sem, recv_sem,
):
    x, y, z, c = place()
    me = (x, y, z)
    vocab, depth = w.shape
    tokens = lt.shape[1]
    partner = device(x, y, z, 1 - c)

    def settle(upto=None):
        upto = len(copies) if upto is None else upto
        for cp in copies[len(settled) : upto]:
            cp.wait_send()
            settled.append(cp)

    def there(moves):
        return device(*[(me[a] + moves.get(a, 0)) % 4 for a in range(3)], c)

    barrier = pltpu.get_barrier_semaphore()
    peers = [partner]
    for d in NEAR:
        peers += [there({axis: d}) for axis in (X, Y, Z)]
        peers += [there({p: d, q: e}) for p, q in ((X, Y), (Y, Z), (X, Z)) for e in NEAR]
    for to in peers:
        pl.semaphore_signal(barrier, inc=1, device_id=to, device_id_type=MESH)
    own_g = (c,) + region(me)
    pairs = [
        (hid_hbm.at[:, pl.ds(0, 128)], g.at[own_g + (pl.ds(0, 64),)]),
        (hid_hbm.at[:, pl.ds(128, 128)], g.at[own_g + (pl.ds(64, 64),)]),
        (tgt_hbm, tgt_ref), (lg_hbm, lg_ref), (w_hbm, w),
    ]
    loads = [pltpu.make_async_copy(a, b, local_sem.at[i]) for i, (a, b) in enumerate(pairs)]
    for cp in loads:
        cp.start()
    lt[...] = jnp.zeros_like(lt)
    for cp in loads[:4]:
        cp.wait()
    pl.semaphore_wait(barrier, len(peers))

    copies, settled = [], []

    def send(src, dst, to):
        i = len(copies)
        cp = pltpu.make_async_remote_copy(
            src, dst, send_sem.at[i], recv_sem.at[i], device_id=to, device_id_type=MESH
        )
        cp.start()
        copies.append(cp)
        return cp

    def spot(k, **at):
        out = [None, None, None]
        for name, axis in zip(("first", "second", "last"), ORDERS[k]):
            d = at.get(name, 0)
            out[axis] = None if d == "all" else (me[axis] + d) % 4
        return tuple(out)

    def spread(k, to, **at):
        ref = g.at[(c,) + region(spot(k, **at), ROWS[k])]
        return send(ref, ref, to)

    got1, got2 = {}, {}
    for s in (0,) + NEAR:
        for k in range(3):
            for d in (0,) + NEAR:
                if s or d:
                    got1[k, s, d] = spread(k, there({ORDERS[k][0]: d, ORDERS[k][1]: s}))
    for s in (0,) + NEAR:
        for k in range(3):
            for d in (0,) + NEAR:
                if s or d:
                    got1[k, s, d].wait_recv()
            for d in NEAR:
                got2[k, s, d] = spread(k, there({ORDERS[k][2]: d}), first="all", second=-s)

    def relay(s):
        done = []
        for k in range(3):
            if k == 0:
                if s:
                    for i in (0,) + NEAR:
                        got2[0, i, s].wait_recv()
            else:
                for d in NEAR:
                    got2[k, s, d].wait_recv()
            ref = g.at[(c,) + region((None, None, (z - s) % 4), ROWS[k])]
            done.append(send(ref, ref, partner))
        return done

    def features(zz, classes=(0, 1)):
        parts = [
            g[cc, :, :, zz, xx, pl.ds(64 * h, 64), :].reshape(tokens, 128)
            for xx in range(2)
            for cc in classes
            for h in range(2)
        ]
        return jnp.concatenate(parts, axis=1)

    def columns(i, width):
        return pl.ds(pl.multiple_of(i * width, width), width)

    def logits(s, cc=None):
        zz = (z - s) % 4
        if cc is None:
            part, rhs = w[:, columns(zz, 1024)], features(zz)
        else:
            part = jnp.concatenate([w[:, columns((zz * 2 + xx) * 2 + cc, 256)] for xx in range(2)], axis=1)
            rhs = features(zz, (cc,))
        lt[...] += lax.dot_general(
            part, rhs, (((1,), (1,)), ((), ())), preferred_element_type=F32
        )

    def arrived(relayed):
        for cp in relayed:
            cp.wait_recv()

    relayed = {0: relay(0)}
    loads[4].wait()
    arrived(relayed[0])
    logits(0)
    for s in NEAR:
        relayed[s] = relay(s)
    logits(1, c)
    arrived(relayed[1])
    logits(1, 1 - c)
    arrived(relayed[3])
    logits(3)
    arrived(relayed[2])
    logits(2)

    s_idx, t_idx = lax.axis_index("section"), lax.axis_index("tensor")
    local = tgt_ref[...] - (s_idx * 16 + t_idx) * vocab
    chunk = 128
    n_chunks = vocab // chunk

    def hit(i):
        ids = lax.broadcasted_iota(jnp.int32, (chunk, tokens), 0) + i * chunk
        return ids == local

    def max_step(i, top):
        return jnp.maximum(top, lt[pl.ds(pl.multiple_of(i * chunk, chunk), chunk), :])

    top = lax.fori_loop(1, n_chunks, max_step, lt[pl.ds(0, chunk), :])
    top = jnp.max(top, axis=0, keepdims=True)

    def exp_step(i, carry):
        total, picked = carry
        rows = pl.ds(pl.multiple_of(i * chunk, chunk), chunk)
        value = lt[rows, :]
        e = jnp.exp(value - top)
        lt[rows, :] = e
        picked = picked + jnp.sum(jnp.where(hit(i), value, 0.0), axis=0, keepdims=True)
        return total + jnp.sum(e, axis=0, keepdims=True), picked

    zero = jnp.zeros((1, tokens), F32)
    total, picked = lax.fori_loop(0, n_chunks, exp_step, (zero, zero))

    for j, v in enumerate((top, total, picked)):
        for i in range(4):
            st_core[0, j, i : i + 1, :] = v[:, 128 * i : 128 * (i + 1)]
    gathered = len(copies)
    send(st_core.at[0], st_core.at[1], partner).wait_recv()
    for j, v in enumerate(combine(st_core[...])):
        st_plane[0, j] = v
    joined = []
    for dx in range(4):
        for dy in range(4):
            i = dx * 4 + dy
            if i:
                joined.append(send(st_plane.at[0], st_plane.at[i], there({X: dx, Y: dy})))
    settle(gathered)
    for cp in joined:
        cp.wait_recv()
    for j, v in enumerate(combine(st_plane[...])):
        st_axis[0, j] = v
    joined = [send(st_axis.at[0], st_axis.at[d], there({Z: d})) for d in NEAR]
    settle(len(copies) - len(joined))
    for cp in joined:
        cp.wait_recv()
    m_all, s_all, p_all = combine(st_axis[...])
    loss_ref[...] = m_all + jnp.log(s_all) - p_all
    lg = lg_ref[...]
    scale = lg * jnp.exp(top - flat(m_all)) / flat(s_all)

    def grad_step(i, _):
        rows = pl.ds(pl.multiple_of(i * chunk, chunk), chunk)
        value = lt[rows, :] * scale - jnp.where(hit(i), lg, 0.0)
        glt[rows, :] = value.astype(BF16)
        return 0

    lax.fori_loop(0, n_chunks, grad_step, 0)
    for i in range(8):
        gl[:, 128 * i : 128 * (i + 1)] = glt[128 * i : 128 * (i + 1), :].T

    def term(zz, xx, cc, out):
        t = (zz * 2 + xx) * 2 + cc
        value = jnp.dot(gl[...], w[:, columns(t, 256)], preferred_element_type=F32)
        value = value.astype(out.dtype)
        out[xx, :, :, 0:64] = value[:, 0:128].reshape(2, 4, 64, 128)
        out[xx, :, :, 64:128] = value[:, 128:256].reshape(2, 4, 64, 128)

    def both(zz, cc, out):
        def step(xx, _):
            term(zz, xx, cc, out)
            return 0

        lax.fori_loop(0, 2, step, 0)

    def swap(i, s):
        both((z + s) % 4, 1 - c, give.at[i])
        return send(give.at[i], take.at[i], partner)

    slots0, slots1 = (a0, b0, c0), (a1, b1, c1)
    finals = (fa, fb, fc)
    red0, red1 = {}, {}

    def reduce_z(s):
        if s:
            ref = r.at[region(spot(0, first="all", second="all", last=s), ROWS[0])]
            red0[0, s] = send(ref, a0.at[s - 1], there({Z: s}))
        for d in NEAR:
            for k in (1, 2):
                ref = r.at[region(spot(k, first="all", second=s, last=d), ROWS[k])]
                red0[k, s, d] = send(ref, slots0[k].at[s, d - 1], there({ORDERS[k][2]: d}))

    def line(k, s):
        ix = region(spot(k, first="all", second=s), ROWS[k])
        value = r[ix].astype(F32)
        for d in NEAR:
            if k == 0:
                value = value + a0[d - 1, :, (y + s) % 4].astype(F32)
            else:
                red0[k, s, d].wait_recv()
                value = value + slots0[k][s, d - 1].astype(F32)
        return ix, value

    def pass_line(k, s):
        ix, value = line(k, s)
        r[ix] = value.astype(BF16)
        if s == 0:
            finals[k][...] = value
        for d in NEAR + (0,):
            if s or d:
                ref = r.at[region(spot(k, first=d, second=s), ROWS[k])]
                to = there({ORDERS[k][0]: d, ORDERS[k][1]: s})
                red1[k, s, d] = send(ref, slots1[k].at[s * 4 + d], to)

    def weight_grad(start, stop):
        def step(i, _):
            for h in range(2):
                rows = slice(512 * h, 512 * (h + 1))
                gw_ref[rows, columns(i, 1024)] = jnp.dot(
                    glt[rows, :], features(i), preferred_element_type=F32
                ).astype(BF16)
            return 0

        lax.fori_loop(start, stop, step, 0)

    turns = NEAR + (0,)
    swaps = [swap(0, turns[0])]
    for i, s in enumerate(turns):
        if i < 3:
            swaps.append(swap(i + 1, turns[i + 1]))
        both((z + s) % 4, c, own)
        swaps[i].wait_recv()
        for xx in range(2):
            r[:, :, (z + s) % 4, xx] = (own[xx] + take[i, xx].astype(F32)).astype(BF16)
        reduce_z(s)
    weight_grad(0, 1)
    reduced = len(copies)
    for k in (1, 2):
        pass_line(k, 1)
    weight_grad(1, 2)
    for k in (1, 2):
        pass_line(k, 3)
    weight_grad(2, 3)
    for d in NEAR:
        red0[0, d].wait_recv()
    for s in NEAR:
        pass_line(0, s)
    pass_line(0, 0)
    for k in (1, 2):
        pass_line(k, 2)
    for k in (1, 2):
        pass_line(k, 0)
    weight_grad(3, 4)
    settle(reduced)
    mine = region(me)
    for k in range(3):
        axis = ORDERS[k][0]
        n = me[axis]
        value = finals[k][(n % 2, n // 2) if axis == X else (n,)]
        for (kk, s, d), cp in red1.items():
            if kk == k:
                cp.wait_recv()
                value = value + slots1[k][s * 4 + d].astype(F32)
        r[region(me, ROWS[k])] = value.astype(BF16)
    gh_ref[:, 0:128] = r[mine + (pl.ds(0, 64),)]
    gh_ref[:, 128:256] = r[mine + (pl.ds(64, 64),)]

    assert len(copies) == COPIES, len(copies)
    settle()


def write_kernel(gw, loss, gh, gw_out, loss_out, gh_out, sem):
    step = gw.shape[0] // PIECES
    pairs = [(gw.at[pl.ds(i * step, step)], gw_out.at[pl.ds(i * step, step)]) for i in range(PIECES)]
    pairs += [(loss, loss_out), (gh, gh_out)]
    copies = [pltpu.make_async_copy(a, b, sem.at[i]) for i, (a, b) in enumerate(pairs)]
    for cp in copies:
        cp.start()
    for cp in copies:
        cp.wait()


def shards(hidden, weight, targets, loss_grad):
    vocab, depth = weight.shape
    tokens = targets.shape[0]
    dma = pltpu.SemaphoreType.DMA
    vmem = pl.BlockSpec(memory_space=pltpu.VMEM)
    anywhere = pl.BlockSpec(memory_space=pl.ANY)
    slot = lambda *s, t=BF16: pltpu.VMEM(s + (128,), t)
    loss, grad_hidden, grad_weight = pl.pallas_call(
        kernel,
        out_shape=(
            pltpu.VMEM((4, 128), F32),
            pltpu.VMEM(hidden.shape, BF16),
            pltpu.VMEM((vocab, depth), BF16),
        ),
        in_specs=[anywhere] * 4,
        out_specs=(vmem, vmem, vmem),
        scratch_shapes=[
            pltpu.VMEM((vocab, depth), BF16),
            pltpu.VMEM((2, 2, 4, 4, 2, 128, 128), BF16),
            pltpu.VMEM((vocab, tokens), F32),
            pltpu.VMEM((vocab, tokens), BF16),
            pltpu.VMEM((tokens, vocab), BF16),
            pltpu.VMEM((2, 2, 4, 128, 128), F32),
            pltpu.VMEM((4, 2, 2, 4, 128, 128), BF16),
            pltpu.VMEM((4, 2, 2, 4, 128, 128), BF16),
            pltpu.VMEM((2, 4, 4, 2, 128, 128), BF16),
            slot(3, 2, 4, 2, 32), slot(4, 3, 4, 48), slot(4, 3, 2, 2, 48),
            slot(16, 32), slot(16, 48), slot(16, 48),
            slot(2, 2, 32, t=F32), slot(4, 48, t=F32), slot(2, 2, 48, t=F32),
            pltpu.VMEM((2, 3, 4, 128), F32),
            pltpu.VMEM((16, 3, 4, 128), F32),
            pltpu.VMEM((4, 3, 4, 128), F32),
            pltpu.VMEM((1, tokens), jnp.int32),
            pltpu.VMEM((1, tokens), F32),
            dma((5,)), dma((COPIES,)), dma((COPIES,)),
        ],
        compiler_params=pltpu.CompilerParams(
            collective_id=0, has_side_effects=True, vmem_limit_bytes=48 * 2**20
        ),
    )(hidden, weight, targets.reshape(1, tokens), loss_grad.reshape(1, tokens))
    grad_weight, loss, grad_hidden = pl.pallas_call(
        write_kernel,
        out_shape=(
            jax.ShapeDtypeStruct((vocab, depth), BF16),
            jax.ShapeDtypeStruct((4, 128), F32),
            jax.ShapeDtypeStruct(hidden.shape, BF16),
        ),
        in_specs=[vmem] * 3,
        out_specs=(anywhere,) * 3,
        scratch_shapes=[dma((PIECES + 2,))],
        compiler_params=pltpu.CompilerParams(vmem_limit_bytes=16 * 2**20),
    )(grad_weight, loss, grad_hidden)
    return loss.reshape(tokens), grad_hidden, grad_weight


def solution(mesh):
    return jax.shard_map(
        shards,
        mesh=mesh,
        in_specs=(P("section", "tensor"), P(("section", "tensor"), None), P(), P()),
        out_specs=(P(), P("section", "tensor"), P(("section", "tensor"), None)),
        check_vma=False,
    )
```
